256 devices in a mesh: fsdp: 64 (over z, x_hi, y), seq: 4 (over x_lo, core).
Axes of the slice: x: 4 (x_hi: 2, x_lo: 2; x = x_hi * 2 + x_lo), y: 4, z: 8, core: 2. Of those that a mesh axis runs over, the one named last changes fastest.
Arguments:
- tokens: bfloat16 [64, 1500, 640], P('fsdp', 'seq'), may hold values from -6 to 6
- cotangent: bfloat16 [64, 1500, 640], P('fsdp', 'seq'), may hold values from -6 to 6
- codes_in: int32 [2560, 640], P(('fsdp', 'seq')), may hold values from 40 to 215, as said below
- scales_in: int32 [2560, 20], P(('fsdp', 'seq')), may hold values from 118 to 122
- codes_out: int32 [2560, 640], P(('fsdp', 'seq')), may hold values from 40 to 215, as said below
- scales_out: int32 [2560, 20], P(('fsdp', 'seq')), may hold values from 118 to 122
- layer_norm_gain: float32 [640], replicated, may hold values from 0.1 to 1.9
- layer_norm_bias: float32 [640], replicated, may hold values from -3 to 3
- bias_in: float32 [2560], replicated, may hold values from -3 to 3
- bias_out: float32 [640], replicated, may hold values from -3 to 3
- master_in: float32 [2560, 640], P(('fsdp', 'seq')), may hold values from -0.25 to 0.25
- moment_in: float32 [2560, 640], P(('fsdp', 'seq')), may hold values from -3 to 3
- second_in: float32 [2560, 640], P(('fsdp', 'seq')), may hold values from 0.01 to 1
- master_out: float32 [2560, 640], P(('fsdp', 'seq')), may hold values from -0.125 to 0.125
- moment_out: float32 [2560, 640], P(('fsdp', 'seq')), may hold values from -3 to 3
- second_out: float32 [2560, 640], P(('fsdp', 'seq')), may hold values from 0.01 to 1
Outputs:
- layer_out: bfloat16 [64, 1500, 640], P('fsdp', 'seq')
- d_tokens: bfloat16 [64, 1500, 640], P('fsdp', 'seq')
- d_gain: float32 [640], replicated
- d_shift: float32 [640], replicated
- d_bias_in: float32 [2560], replicated
- d_bias_out: float32 [640], replicated
- new_master_in: float32 [2560, 640], P(('fsdp', 'seq'))
- new_moment_in: float32 [2560, 640], P(('fsdp', 'seq'))
- new_second_in: float32 [2560, 640], P(('fsdp', 'seq'))
- new_master_out: float32 [2560, 640], P(('fsdp', 'seq'))
- new_moment_out: float32 [2560, 640], P(('fsdp', 'seq'))
- new_second_out: float32 [2560, 640], P(('fsdp', 'seq'))
The draws below stay inside these ranges and needn't reach their ends.
Inputs may be any that keep to these rules, and one draw needn't show every extreme that they name: `codes_in`: each code is 128 times a sign bit plus 8 times an exponent field of 5 to 10 plus a mantissa of 0 to 7. `codes_out`: each code is 128 times a sign bit plus 8 times an exponent field of 5 to 10 plus a mantissa of 0 to 7.
All inputs are finite; a program needn't handle non-finite values.
Results may differ from the reference program's by a relative error of at most 0.013.
Values may be sent and summed in bfloat16 or wider, within the bound.
A program may use at most 128 MiB of HBM per device.

```python
import math
import jax
import jax.numpy as jnp
from jax import lax

D = 640
FF = 2560
FRAMES = 1500
CLIPS = 64
TOKENS = 96000


def draw_fields(key, shape):
    sign_bit = jax.random.randint(jax.random.fold_in(key, 11), shape, 0, 2)
    expo_field = jax.random.randint(jax.random.fold_in(key, 12), shape, 5, 11)
    mant_field = jax.random.randint(jax.random.fold_in(key, 13), shape, 0, 8)
    return (sign_bit * 128 + expo_field * 8 + mant_field).astype(jnp.int32)


def draw_codes_in(key, part):
    key = jax.random.fold_in(key, 3)
    return draw_fields(key, (FF, D))


def draw_codes_out(key, part):
    key = jax.random.fold_in(key, 5)
    return draw_fields(key, (FF, D))


def place_ends(result, own_key, smallest, top_value):
    shape = result.shape
    spot = [jax.random.randint(jax.random.fold_in(own_key, axis), (), 0, shape[axis]) for axis in range(len(shape))]
    result = result.at[tuple(spot)].set(smallest)
    longest = shape.index(max(shape))
    spot[longest] = (spot[longest] + 1) % shape[longest]
    return result.at[tuple(spot)].set(top_value)


def level_of(stream_key, dims, cuts, least, largest):
    factor_of = 1.0
    for dim, blocks in cuts:
        steps = jax.random.uniform(jax.random.fold_in(jax.random.fold_in(stream_key, 6), dim), (blocks,), jnp.float32, least / len(cuts), largest / len(cuts))
        factor_of = factor_of * jnp.repeat(jnp.exp(steps), dims[dim] // blocks).reshape((-1,) + (1,) * (len(dims) - 1 - dim))
    return factor_of


def normal_values(stream_key, extent, spread, most, pieces=(), dtype=jnp.bfloat16):
    result = jax.random.normal(stream_key, extent, jnp.float32) * spread
    if len(pieces) > 0:
        result = level_of(stream_key, extent, pieces, -0.22, 0.18) * result
    return jnp.clip(result, min=-most, max=most).astype(dtype)


def setup_inputs(seed: int = 0) -> dict:
    splits = jax.random.split(jax.random.key(seed), 17)
    tokens = normal_values(splits[0], (CLIPS, FRAMES, D), 1.0, 6.0, ((0, 64), (1, 4)))
    cotangent = normal_values(splits[1], (CLIPS, FRAMES, D), 1.0, 6.0, ((0, 64), (1, 4)))
    codes_in = draw_codes_in(jax.random.fold_in(splits[16], 71), 0)
    scales_in = place_ends(jax.random.randint(splits[3], (FF, D // 32), 118, 123), jax.random.fold_in(splits[3], 1), 118, 122).astype(jnp.int32)
    codes_out = draw_codes_out(jax.random.fold_in(splits[16], 71), 0)
    scales_out = place_ends(jax.random.randint(splits[5], (FF, D // 32), 118, 123), jax.random.fold_in(splits[5], 1), 118, 122).astype(jnp.int32)
    layer_norm_gain = jnp.clip(1.0 + 0.18 * jax.random.normal(splits[6], (D,), jnp.float32), 0.1, 1.9)
    layer_norm_bias = normal_values(splits[7], (D,), 0.5, 3.0, (), jnp.float32)
    bias_in = normal_values(splits[8], (FF,), 0.5, 3.0, (), jnp.float32)
    bias_out = normal_values(splits[9], (D,), 0.5, 3.0, (), jnp.float32)
    master_in = normal_values(splits[10], (FF, D), D ** -0.5, 0.25, ((0, 256),), jnp.float32)
    moment_in = normal_values(splits[11], (FF, D), 0.5, 3.0, ((0, 256),), jnp.float32)
    second_in = jnp.clip(jnp.exp(math.log(1.0) - 4.6051702 * jax.random.uniform(splits[12], (FF, D), jnp.float32) ** level_of(splits[12], (FF, D), ((0, 256),), -0.2, 0.2)), 0.01, 1.0)
    master_out = normal_values(splits[13], (FF, D), FF ** -0.5, 0.125, ((0, 256),), jnp.float32)
    moment_out = normal_values(splits[14], (FF, D), 0.5, 3.0, ((0, 256),), jnp.float32)
    second_out = jnp.clip(jnp.exp(math.log(1.0) - 4.6051702 * jax.random.uniform(splits[15], (FF, D), jnp.float32) ** level_of(splits[15], (FF, D), ((0, 256),), -0.2, 0.2)), 0.01, 1.0)
    return dict(tokens=tokens, cotangent=cotangent, codes_in=codes_in, scales_in=scales_in, codes_out=codes_out, scales_out=scales_out, layer_norm_gain=layer_norm_gain, layer_norm_bias=layer_norm_bias, bias_in=bias_in, bias_out=bias_out, master_in=master_in, moment_in=moment_in, second_in=second_in, master_out=master_out, moment_out=moment_out, second_out=second_out)


def decode(codes, scales):
    sign_bit = (codes // 128).astype(jnp.float32)
    expo_field = codes // 8 % 16
    mant_field = (codes % 8).astype(jnp.float32)
    normal_mag = jnp.exp2(expo_field.astype(jnp.float32) - 7.0) * (1.0 + mant_field / 8.0)
    small_mag = mant_field * 2.0 ** (-9)
    values = (1.0 - 2.0 * sign_bit) * jnp.where(expo_field > 0, normal_mag, small_mag)
    blocks = jnp.exp2(scales.astype(jnp.float32) - 127.0)
    row_count, col_count = codes.shape
    scaled = values.reshape(row_count, col_count // 32, 32) * blocks[:, :, None]
    return scaled.reshape(row_count, col_count).astype(jnp.bfloat16)

def gelu_slope(values):
    return 0.5 * (1.0 + lax.erf(values * 0.7071067811865476)) + values * jnp.exp(-0.5 * values * values) * 0.3989422804014327

def contraction_rows(left, right):
    return lax.dot_general(left, right, (((0,), (0,)), ((), ())), preferred_element_type=jnp.float32)

def contract_cols(left, right):
    return lax.dot_general(left, right, (((1,), (1,)), ((), ())), preferred_element_type=jnp.float32)

def adamw(master, moment, second, grad):
    new_moment = 0.9 * moment + 0.1 * grad
    new_second = 0.95 * second + 0.05 * grad * grad
    new_master = master - 0.001 * (new_moment / (jnp.sqrt(new_second) + 1e-08) + 0.1 * master)
    return (new_master, new_moment, new_second)

def reference(tokens, cotangent, codes_in, scales_in, codes_out, scales_out, layer_norm_gain, layer_norm_bias, bias_in, bias_out, master_in, moment_in, second_in, master_out, moment_out, second_out):
    w_in = decode(codes_in, scales_in)
    w_out = decode(codes_out, scales_out)

    def clip_step(loop_state, item):
        tok_rows, cotangent_rows = item
        tok_float = tok_rows.astype(jnp.float32)
        mean_removed = tok_float - lax.optimization_barrier(jnp.mean(tok_float, axis=-1, keepdims=True))
        inverse_deviation = lax.rsqrt(lax.optimization_barrier(jnp.mean(mean_removed * mean_removed, axis=-1, keepdims=True)) + 1e-05)
        standardized_tokens = mean_removed * inverse_deviation
        normalized_tokens = (standardized_tokens * layer_norm_gain + layer_norm_bias).astype(jnp.bfloat16)
        pre = contract_cols(normalized_tokens, w_in) + bias_in
        gelu_output = jax.nn.gelu(pre, approximate=False).astype(jnp.bfloat16)
        layer = (tok_float + jnp.dot(gelu_output, w_out, preferred_element_type=jnp.float32) + bias_out).astype(jnp.bfloat16)
        cotangent_float = cotangent_rows.astype(jnp.float32)
        preactivation_gradient = (contract_cols(cotangent_rows, w_out) * gelu_slope(pre)).astype(jnp.bfloat16)
        normalized_gradient = jnp.dot(preactivation_gradient, w_in, preferred_element_type=jnp.float32)
        standardized_gradient = normalized_gradient * layer_norm_gain
        token_gradient = (cotangent_float + inverse_deviation * (standardized_gradient - lax.optimization_barrier(jnp.mean(standardized_gradient, axis=-1, keepdims=True)) - standardized_tokens * lax.optimization_barrier(jnp.mean(standardized_gradient * standardized_tokens, axis=-1, keepdims=True)))).astype(jnp.bfloat16)
        input_weight_gradient, output_weight_gradient, norm_gain_gradient, norm_bias_gradient, input_bias_gradient, output_bias_gradient = loop_state
        loop_state = (input_weight_gradient + contraction_rows(preactivation_gradient, normalized_tokens), output_weight_gradient + contraction_rows(gelu_output, cotangent_rows), norm_gain_gradient + lax.optimization_barrier(jnp.sum(normalized_gradient * standardized_tokens, axis=0)), norm_bias_gradient + lax.optimization_barrier(jnp.sum(normalized_gradient, axis=0)), input_bias_gradient + lax.optimization_barrier(jnp.sum(preactivation_gradient.astype(jnp.float32), axis=0)), output_bias_gradient + lax.optimization_barrier(jnp.sum(cotangent_float, axis=0)))
        return (loop_state, (layer, token_gradient))
    width = tokens.shape[2]
    hidden = w_in.shape[0]
    start = (jnp.zeros((hidden, width), jnp.float32), jnp.zeros((hidden, width), jnp.float32), jnp.zeros((width,), jnp.float32), jnp.zeros((width,), jnp.float32), jnp.zeros((hidden,), jnp.float32), jnp.zeros((width,), jnp.float32))
    sums, outs = lax.scan(clip_step, start, (tokens, cotangent))
    layer_out, d_tokens = outs
    reduction_factor = 1.0 / math.sqrt(TOKENS)
    grad_in, grad_out, d_gain, d_shift, d_bias_in, d_bias_out = [part * reduction_factor for part in sums]
    new_master_in, new_moment_in, new_second_in = adamw(master_in, moment_in, second_in, grad_in)
    new_master_out, new_moment_out, new_second_out = adamw(master_out, moment_out, second_out, grad_out)
    return (layer_out, d_tokens, d_gain, d_shift, d_bias_in, d_bias_out, new_master_in, new_moment_in, new_second_in, new_master_out, new_moment_out, new_second_out)
```

```python
import math

import jax
import jax.numpy as jnp
from jax import lax
from jax.experimental import pallas as pl
from jax.experimental.pallas import tpu as pltpu
from jax.sharding import PartitionSpec as P

NX, NY, NZ, NC = 4, 4, 8, 2
WIDTH = 640
OWN = 10
FRAMES = 375
ROWS = 384
CHUNK = NZ * OWN
BLOCK = NX * CHUNK
HIDDEN = NY * BLOCK
SHARD = 32
TOKENS = 96000
BF, F32 = jnp.bfloat16, jnp.float32
MESH = pl.DeviceIdType.MESH


def dot_nn(a, b):
    return jnp.dot(a, b, preferred_element_type=F32)


def dot_nt(a, b):
    return lax.dot_general(a, b, (((1,), (1,)), ((), ())), preferred_element_type=F32)


def dot_tn(a, b):
    return lax.dot_general(a, b, (((0,), (0,)), ((), ())), preferred_element_type=F32)


def coordinates():
    f = lax.axis_index("fsdp")
    s = lax.axis_index("seq")
    y = lax.rem(f, 4)
    x_hi = lax.rem(f // 4, 2)
    return x_hi * 2 + s // 2, y, f // 8, lax.rem(s, 2)


def device(x, y, z, c):
    return ((z * 2 + x // 2) * 4 + y, lax.rem(x, 2) * 2 + c)


def decode(codes, scales):
    spread = (
        lax.broadcasted_iota(jnp.int32, (20, WIDTH), 1) // 32
        == lax.broadcasted_iota(jnp.int32, (20, WIDTH), 0)
    )
    k = dot_nn((scales - 118).astype(F32).astype(BF), spread.astype(F32).astype(BF)).astype(jnp.int32)
    negative = codes >= 128
    e = (codes >> 3) & 15
    m = codes & 7
    whole = jnp.where(e > 0, m + 8, m)
    value = (whole << (jnp.maximum(e, 1) + k - 1)).astype(F32) * (2.0**-18)
    return jnp.where(negative, -value, value)


def shard_select():
    r = lax.broadcasted_iota(jnp.int32, (2 * CHUNK, NZ * SHARD), 0)
    col = lax.broadcasted_iota(jnp.int32, (2 * CHUNK, NZ * SHARD), 1)
    second = (r >= CHUNK).astype(jnp.int32)
    r = r - CHUNK * second
    z = jnp.zeros_like(r)
    for j in range(1, NZ):
        z = z + (r >= OWN * j).astype(jnp.int32)
    return (col == z * (SHARD - OWN) + r + 16 * second).astype(F32).astype(BF)


def adamw(master, moment, second, grad):
    new_moment = 0.9 * moment + 0.1 * grad
    new_second = 0.95 * second + 0.05 * grad * grad
    new_master = master - 0.001 * (new_moment / (jnp.sqrt(new_second) + 1e-08) + 0.1 * master)
    return new_master, new_moment, new_second


def kernel(
    tok_ref, cot_ref, cin_ref, sin_ref, cout_ref, sout_ref,
    gain_ref, shift_ref, bin_ref, bout_ref,
    min_ref, vin_ref, qin_ref, mout_ref, vout_ref, qout_ref,
    layer_ref, dtok_ref, vec_ref,
    omin_ref, ovin_ref, oqin_ref, omout_ref, ovout_ref, oqout_ref,
    tokb, cotb, normed, xhat, rstd, shard, zbuf, win, wout, bcol, dbp, act, dpre,
    gin, gout, r1in, r1out, s1in, s1out, r2in, r2out, zsend, r3,
    part, partr, vown, vcore, vy, vx, vz,
    cs, cr, zs, zr, a2s, a2r, a3s, a3r, g1is, g1ir, g1os, g1or, g2s, g2r, g3s, g3r, ps, pr, vs, vr,
):
    x, y, z, c = coordinates()
    xp = [lax.rem(x + d, NX) for d in range(NX)]
    yp = [lax.rem(y + d, NY) for d in range(NY)]
    zp = [lax.rem(z + d, NZ) for d in range(NZ)]
    to_x = [device(q, y, z, c) for q in xp]
    to_y = [device(x, q, z, c) for q in yp]
    to_z = [device(x, y, q, c) for q in zp]
    to_c = device(x, y, z, 1 - c)
    pending = []

    def send(src, dst, ssem, rsem, target):
        copy = pltpu.make_async_remote_copy(
            src_ref=src, dst_ref=dst, send_sem=ssem, recv_sem=rsem,
            device_id=target, device_id_type=MESH,
        )
        copy.start()
        pending.append(copy)
        return copy

    barrier = pltpu.get_barrier_semaphore()
    for q in to_x[1:] + to_y[1:] + to_z[1:] + [to_c]:
        pl.semaphore_signal(barrier, inc=1, device_id=q, device_id_type=MESH)

    shard[...] = jnp.zeros_like(shard)
    shard[0:OWN, :] = decode(cin_ref[...], sin_ref[...]).astype(BF)
    shard[16 : 16 + OWN, :] = decode(cout_ref[...], sout_ref[...]).astype(BF)
    zbuf[z] = shard[...]
    for buf, ref in ((tokb, tok_ref), (cotb, cot_ref)):
        buf[ROWS - 16 : ROWS, :] = jnp.zeros((16, WIDTH), BF)
        buf[0:FRAMES, :] = ref[0]
    pl.semaphore_wait(barrier, NX + NY + NZ - 2)

    zc = [
        send(shard, zbuf.at[z], zs.at[d - 1], zr.at[d - 1], to_z[d])
        for d in (4, 3, 5, 2, 6, 1, 7)
    ]
    own, other = slice(0, ROWS), slice(ROWS, 2 * ROWS)
    cc = [
        send(buf.at[own], buf.at[other], cs.at[i], cr.at[i], to_c)
        for i, buf in enumerate((tokb, cotb))
    ]

    def norm(rows):
        t = tokb[rows, :].astype(F32)
        t = t - jnp.mean(t, axis=-1, keepdims=True)
        inv = lax.rsqrt(jnp.mean(t * t, axis=-1, keepdims=True) + 1e-05)
        t = t * inv
        normed[rows, :] = (t * gain_ref[...] + shift_ref[...]).astype(BF)
        return t, inv

    t, inv = norm(own)
    xhat[...] = t
    rstd[...] = inv
    bias = jnp.where(c == 0, bin_ref[0:1, :], bin_ref[1:2, :])
    bcol[...] = jnp.transpose(jnp.broadcast_to(bias, (128, HIDDEN)))
    select = shard_select()
    for copy in cc:
        copy.wait_recv()
    norm(other)

    for copy in zc:
        copy.wait_recv()
    w = dot_nn(select, zbuf[...].reshape(NZ * SHARD, WIDTH)).astype(BF)
    win[y, x] = w[:CHUNK]
    wout[y, x] = w[CHUNK:]

    def second(d):
        return (
            send(win.at[y, x], win.at[y, x], a2s.at[0, d - 1], a2r.at[0, d - 1], to_x[d]),
            send(wout.at[y, x], wout.at[y, x], a2s.at[1, d - 1], a2r.at[1, d - 1], to_y[d]),
        )

    def third(d):
        fx, fy = lax.rem(x + NX - d, NX), lax.rem(y + NY - d, NY)
        out = []
        for e in (1, 3, 2):
            out.append(send(win.at[y, fx], win.at[y, fx], a3s.at[0, d, e - 1], a3r.at[0, d, e - 1], to_y[e]))
            out.append(send(wout.at[fy, x], wout.at[fy, x], a3s.at[1, d, e - 1], a3r.at[1, d, e - 1], to_x[e]))
        return out

    c2 = {d: second(d) for d in (1, 3, 2)}
    c3 = third(0)
    for d in (1, 3, 2):
        for copy in c2[d]:
            copy.wait_recv()
        c3 += third(d)
    for copy in c3:
        copy.wait_recv()

    g1i, g1o = [], []
    for d in (1, 3, 2, 0):
        by = yp[d]
        rows = pl.ds(pl.multiple_of(by * BLOCK, BLOCK), BLOCK)
        v = dot_nt(win[by].reshape(BLOCK, WIDTH), normed[...]) + bcol[rows, 0:1]
        phi = 0.5 * (1.0 + lax.erf(v * 0.7071067811865476))
        slope = phi + v * jnp.exp(-0.5 * v * v) * 0.3989422804014327
        a = (v * phi).astype(BF)
        act[rows, :] = a
        dp = dot_nt(wout[by].reshape(BLOCK, WIDTH), cotb[...]) * slope
        folded = dp[:, 0:128]
        for j in range(1, 6):
            folded = folded + dp[:, 128 * j : 128 * j + 128]
        dbp[rows, :] = folded
        dp = dp.astype(BF)
        dpre[rows, :] = dp
        gin[by] = dot_nn(dp, normed[...]).astype(BF).reshape(NX, CHUNK, WIDTH)
        if d:
            g1i.append(send(gin.at[by], r1in.at[d - 1], g1is.at[d - 1], g1ir.at[d - 1], to_y[d]))
        gout[by] = dot_nn(a, cotb[...]).astype(BF).reshape(NX, CHUNK, WIDTH)
        for e in (1, 3, 2):
            g1o.append(
                send(gout.at[by, xp[e]], r1out.at[e - 1, by], g1os.at[d, e - 1], g1or.at[d, e - 1], to_x[e])
            )

    wi = win[...].reshape(HIDDEN, WIDTH)
    wo = wout[...].reshape(HIDDEN, WIDTH)
    pc = []
    part[0, 1] = dot_tn(act[:, other], wo)
    pc.append(send(part.at[0, 1], partr.at[0], ps.at[0], pr.at[0], to_c))
    part[1, 1] = dot_tn(dpre[:, other], wi)
    pc.append(send(part.at[1, 1], partr.at[1], ps.at[1], pr.at[1], to_c))
    part[0, 0] = dot_tn(act[:, own], wo)
    part[1, 0] = dot_tn(dpre[:, own], wi)
    cot = cotb[own, :].astype(F32)
    pc[0].wait_recv()
    layer = tokb[own, :].astype(F32) + (part[0, 0] + partr[0]) + bout_ref[...]
    layer_ref[0] = layer.astype(BF)[0:FRAMES]
    pc[1].wait_recv()
    dn = part[1, 0] + partr[1]
    xh = xhat[...]
    dx = dn * gain_ref[...]
    dt = cot + rstd[...] * (
        dx - jnp.mean(dx, axis=-1, keepdims=True) - xh * jnp.mean(dx * xh, axis=-1, keepdims=True)
    )
    dtok_ref[0] = dt.astype(BF)[0:FRAMES]

    db = jnp.sum(jnp.transpose(dbp[...]), axis=0, keepdims=True)
    zero = jnp.zeros_like(db)
    db0, db1 = jnp.where(c == 0, db, zero), jnp.where(c == 0, zero, db)
    vown[0:1, :] = db0[:, 0:WIDTH]
    vown[1:2, :] = db0[:, WIDTH:]
    vown[2:3, :] = db1[:, 0:WIDTH]
    vown[3:4, :] = db1[:, WIDTH:]
    vown[4:5, :] = jnp.sum(dn * xh, axis=0, keepdims=True)
    vown[5:6, :] = jnp.sum(dn, axis=0, keepdims=True)
    vown[6:7, :] = jnp.sum(cot, axis=0, keepdims=True)
    vown[7:8, :] = jnp.zeros((1, WIDTH), F32)
    vc = send(vown, vcore, vs.at[0], vr.at[0], to_c)
    vc.wait_recv()
    vy[y] = vown[...] + vcore[...]
    vyc = [send(vy.at[y], vy.at[y], vs.at[d], vr.at[d], to_y[d]) for d in (1, 3, 2)]

    def add_in():
        for copy in g1i:
            copy.wait_recv()
        for q in range(NX):
            total = gin[y, q].astype(F32)
            for d in range(3):
                total = total + r1in[d, q].astype(F32)
            s1in[q] = total.astype(BF)

    def add_out():
        for copy in g1o:
            copy.wait_recv()
        for q in range(NY):
            total = gout[q, x].astype(F32)
            for d in range(3):
                total = total + r1out[d, q].astype(F32)
            s1out[q] = total.astype(BF)

    add_in()
    g2 = [send(s1in.at[xp[d]], r2in.at[d - 1], g2s.at[0, d - 1], g2r.at[0, d - 1], to_x[d]) for d in (1, 3, 2)]
    add_out()
    g2 += [send(s1out.at[yp[d]], r2out.at[d - 1], g2s.at[1, d - 1], g2r.at[1, d - 1], to_y[d]) for d in (1, 3, 2)]
    for copy in vyc:
        copy.wait_recv()
    vx[x] = (vy[0] + vy[1]) + (vy[2] + vy[3])
    vxc = [send(vx.at[x], vx.at[x], vs.at[3 + d], vr.at[3 + d], to_x[d]) for d in (1, 3, 2)]

    for copy in g2:
        copy.wait_recv()
    sums = []
    for first, got in ((s1in[x], r2in), (s1out[y], r2out)):
        total = first.astype(F32)
        for d in range(3):
            total = total + got[d].astype(F32)
        sums.append(total.astype(BF))
    both = jnp.concatenate(sums, axis=0)
    zsend[...] = dot_tn(select, both).astype(BF).reshape(NZ, SHARD, WIDTH)
    g3 = [
        send(zsend.at[zp[d]], r3.at[d - 1], g3s.at[d - 1], g3r.at[d - 1], to_z[d])
        for d in (4, 3, 5, 2, 6, 1, 7)
    ]
    for copy in vxc:
        copy.wait_recv()
    vz[z] = (vx[0] + vx[1]) + (vx[2] + vx[3])
    vzc = [send(vz.at[z], vz.at[z], vs.at[6 + d], vr.at[6 + d], to_z[d]) for d in (4, 3, 5, 2, 6, 1, 7)]

    for copy in g3:
        copy.wait_recv()
    grad = zsend[z].astype(F32)
    for d in range(NZ - 1):
        grad = grad + r3[d].astype(F32)
    grad = grad * (1.0 / math.sqrt(TOKENS))
    omin_ref[...], ovin_ref[...], oqin_ref[...] = adamw(
        min_ref[...], vin_ref[...], qin_ref[...], grad[0:OWN]
    )
    omout_ref[...], ovout_ref[...], oqout_ref[...] = adamw(
        mout_ref[...], vout_ref[...], qout_ref[...], grad[16 : 16 + OWN]
    )
    for copy in vzc:
        copy.wait_recv()
    total = vz[0]
    for q in range(1, NZ):
        total = total + vz[q]
    vec_ref[...] = total * (1.0 / math.sqrt(TOKENS))
    for copy in pending:
        copy.wait_send()


def body(
    tokens, cotangent, codes_in, scales_in, codes_out, scales_out,
    layer_norm_gain, layer_norm_bias, bias_in, bias_out,
    master_in, moment_in, second_in, master_out, moment_out, second_out,
):
    bias = bias_in.reshape(NZ, 2, NY, 2, NC, OWN).transpose(4, 2, 1, 3, 0, 5).reshape(NC, HIDDEN)
    vmem = pl.BlockSpec(memory_space=pltpu.VMEM)
    owned = jax.ShapeDtypeStruct((OWN, WIDTH), F32)
    dma = pltpu.SemaphoreType.DMA
    outs = pl.pallas_call(
        kernel,
        out_shape=[
            jax.ShapeDtypeStruct(tokens.shape, BF),
            jax.ShapeDtypeStruct(tokens.shape, BF),
            jax.ShapeDtypeStruct((8, WIDTH), F32),
        ]
        + [owned] * 6,
        in_specs=[vmem] * 16,
        out_specs=[vmem] * 9,
        scratch_shapes=[
            pltpu.VMEM((2 * ROWS, WIDTH), BF),
            pltpu.VMEM((2 * ROWS, WIDTH), BF),
            pltpu.VMEM((2 * ROWS, WIDTH), BF),
            pltpu.VMEM((ROWS, WIDTH), F32),
            pltpu.VMEM((ROWS, 1), F32),
            pltpu.VMEM((SHARD, WIDTH), BF),
            pltpu.VMEM((NZ, SHARD, WIDTH), BF),
            pltpu.VMEM((NY, NX, CHUNK, WIDTH), BF),
            pltpu.VMEM((NY, NX, CHUNK, WIDTH), BF),
            pltpu.VMEM((HIDDEN, 128), F32),
            pltpu.VMEM((HIDDEN, 128), F32),
            pltpu.VMEM((HIDDEN, 2 * ROWS), BF),
            pltpu.VMEM((HIDDEN, 2 * ROWS), BF),
            pltpu.VMEM((NY, NX, CHUNK, WIDTH), BF),
            pltpu.VMEM((NY, NX, CHUNK, WIDTH), BF),
            pltpu.VMEM((NY - 1, NX, CHUNK, WIDTH), BF),
            pltpu.VMEM((NX - 1, NY, CHUNK, WIDTH), BF),
            pltpu.VMEM((NX, CHUNK, WIDTH), BF),
            pltpu.VMEM((NY, CHUNK, WIDTH), BF),
            pltpu.VMEM((NX - 1, CHUNK, WIDTH), BF),
            pltpu.VMEM((NY - 1, CHUNK, WIDTH), BF),
            pltpu.VMEM((NZ, SHARD, WIDTH), BF),
            pltpu.VMEM((NZ - 1, SHARD, WIDTH), BF),
            pltpu.VMEM((2, 2, ROWS, WIDTH), F32),
            pltpu.VMEM((2, ROWS, WIDTH), F32),
            pltpu.VMEM((8, WIDTH), F32),
            pltpu.VMEM((8, WIDTH), F32),
            pltpu.VMEM((NY, 8, WIDTH), F32),
            pltpu.VMEM((NX, 8, WIDTH), F32),
            pltpu.VMEM((NZ, 8, WIDTH), F32),
            dma((2,)), dma((2,)),
            dma((7,)), dma((7,)),
            dma((2, 3)), dma((2, 3)),
            dma((2, 4, 3)), dma((2, 4, 3)),
            dma((3,)), dma((3,)),
            dma((4, 3)), dma((4, 3)),
            dma((2, 3)), dma((2, 3)),
            dma((7,)), dma((7,)),
            dma((2,)), dma((2,)),
            dma((14,)), dma((14,)),
        ],
        compiler_params=pltpu.CompilerParams(
            collective_id=0, has_side_effects=True, vmem_limit_bytes=56 * 2**20
        ),
    )(
        tokens, cotangent, codes_in, scales_in, codes_out, scales_out,
        layer_norm_gain.reshape(1, WIDTH), layer_norm_bias.reshape(1, WIDTH),
        bias, bias_out.reshape(1, WIDTH),
        master_in, moment_in, second_in, master_out, moment_out, second_out,
    )
    layer, d_tokens, vec = outs[:3]
    d_bias_in = (
        vec[0:4].reshape(NC, NY, 2, 2, NZ, OWN).transpose(4, 2, 1, 3, 0, 5).reshape(NC * HIDDEN)
    )
    return (layer, d_tokens, vec[4], vec[5], d_bias_in, vec[6]) + tuple(outs[3:])


def solution(mesh):
    tokens, rows, whole = P("fsdp", "seq", None), P(("fsdp", "seq"), None), P()
    return jax.shard_map(
        body,
        mesh=mesh,
        in_specs=(tokens,) * 2 + (rows,) * 4 + (whole,) * 4 + (rows,) * 6,
        out_specs=(tokens,) * 2 + (whole,) * 4 + (rows,) * 6,
        check_vma=False,
    )
```

```python
import math

import jax
import jax.numpy as jnp
from jax import lax
from jax.experimental import pallas as pl
from jax.experimental.pallas import tpu as pltpu
from jax.sharding import PartitionSpec as P

NX, NY, NZ, NC = 4, 4, 8, 2
WIDTH = 640
OWN = 10
FRAMES = 375
ROWS = 384
CHUNK = NZ * OWN
BLOCK = NX * CHUNK
HIDDEN = NY * BLOCK
SHARD = 32
TOKENS = 96000
BF, F32 = jnp.bfloat16, jnp.float32
MESH = pl.DeviceIdType.MESH


def dot_nn(a, b):
    return jnp.dot(a, b, preferred_element_type=F32)


def dot_nt(a, b):
    return lax.dot_general(a, b, (((1,), (1,)), ((), ())), preferred_element_type=F32)


def dot_tn(a, b):
    return lax.dot_general(a, b, (((0,), (0,)), ((), ())), preferred_element_type=F32)


def coordinates():
    f = lax.axis_index("fsdp")
    s = lax.axis_index("seq")
    y = lax.rem(f, 4)
    x_hi = lax.rem(f // 4, 2)
    return x_hi * 2 + s // 2, y, f // 8, lax.rem(s, 2)


def device(x, y, z, c):
    return ((z * 2 + x // 2) * 4 + y, lax.rem(x, 2) * 2 + c)


def decode(codes, scales):
    spread = (
        lax.broadcasted_iota(jnp.int32, (20, WIDTH), 1) // 32
        == lax.broadcasted_iota(jnp.int32, (20, WIDTH), 0)
    )
    k = dot_nn((scales - 118).astype(F32).astype(BF), spread.astype(F32).astype(BF)).astype(jnp.int32)
    negative = codes >= 128
    e = (codes >> 3) & 15
    m = codes & 7
    whole = jnp.where(e > 0, m + 8, m)
    value = (whole << (jnp.maximum(e, 1) + k - 1)).astype(F32) * (2.0**-18)
    return jnp.where(negative, -value, value)


def shard_select():
    r = lax.broadcasted_iota(jnp.int32, (2 * CHUNK, NZ * SHARD), 0)
    col = lax.broadcasted_iota(jnp.int32, (2 * CHUNK, NZ * SHARD), 1)
    second = (r >= CHUNK).astype(jnp.int32)
    r = r - CHUNK * second
    z = jnp.zeros_like(r)
    for j in range(1, NZ):
        z = z + (r >= OWN * j).astype(jnp.int32)
    return (col == z * (SHARD - OWN) + r + 16 * second).astype(F32).astype(BF)


def order_mask():
    j = lax.broadcasted_iota(jnp.int32, (128, WIDTH), 1)
    later = (j >= 320).astype(jnp.int32)
    j = j - 320 * later
    group = (j * 6554) >> 16
    return group, later * OWN + j - OWN * group


def group_of(xx, yy, c):
    return ((xx // 2 * 4 + yy) * 2 + xx % 2) * 2 + c


def dot_exact(a, b, dims):
    return lax.dot_general(
        a, b, (dims, ((), ())), preferred_element_type=F32, precision=lax.Precision.HIGHEST
    )


def adamw(master, moment, second, grad):
    new_moment = 0.9 * moment + 0.1 * grad
    new_second = 0.95 * second + 0.05 * grad * grad
    new_master = master - 0.001 * (new_moment / (jnp.sqrt(new_second) + 1e-08) + 0.1 * master)
    return new_master, new_moment, new_second


def kernel(
    tok_ref, cot_ref, cin_ref, sin_ref, cout_ref, sout_ref,
    gain_ref, shift_ref, bin_ref, bout_ref,
    layer_ref, dtok_ref, vec_ref, grad_ref,
    tokb, cotb, normed, xhat, rstd, shard, zbuf, win, wout, bcol, dbp, act, dpre,
    gin, gout, r1in, r1out, s1in, s1out, r2in, r2out, zsend, r3,
    part, partr, vown, vcore, vy, vx, vz,
    cs, cr, zs, zr, ws, wr, g1is, g1ir, g1os, g1or, g2s, g2r, g3s, g3r, ps, pr, vs, vr,
):
    x, y, z, c = coordinates()
    xp = [lax.rem(x + d, NX) for d in range(NX)]
    yp = [lax.rem(y + d, NY) for d in range(NY)]
    zp = [lax.rem(z + d, NZ) for d in range(NZ)]
    to_x = [device(q, y, z, c) for q in xp]
    to_y = [device(x, q, z, c) for q in yp]
    to_z = [device(x, y, q, c) for q in zp]
    to_c = device(x, y, z, 1 - c)
    pending = []

    def send(src, dst, ssem, rsem, target):
        copy = pltpu.make_async_remote_copy(
            src_ref=src, dst_ref=dst, send_sem=ssem, recv_sem=rsem,
            device_id=target, device_id_type=MESH,
        )
        copy.start()
        pending.append(copy)
        return copy

    barrier = pltpu.get_barrier_semaphore()
    for q in to_x[1:] + to_y[1:] + to_z[1:] + [to_c]:
        pl.semaphore_signal(barrier, inc=1, device_id=q, device_id_type=MESH)

    shard[...] = jnp.zeros_like(shard)
    shard[0:OWN, :] = decode(cin_ref[...], sin_ref[...]).astype(BF)
    shard[16 : 16 + OWN, :] = decode(cout_ref[...], sout_ref[...]).astype(BF)
    zbuf[z] = shard[...]
    for buf, ref in ((tokb, tok_ref), (cotb, cot_ref)):
        buf[ROWS - 16 : ROWS, :] = jnp.zeros((16, WIDTH), BF)
        buf[0:FRAMES, :] = ref[0]
    pl.semaphore_wait(barrier, NX + NY + NZ - 2)

    zc = [
        send(shard, zbuf.at[z], zs.at[d - 1], zr.at[d - 1], to_z[d])
        for d in (4, 3, 5, 2, 6, 1, 7)
    ]
    own, other = slice(0, ROWS), slice(ROWS, 2 * ROWS)
    cc = [
        send(buf.at[own], buf.at[other], cs.at[i], cr.at[i], to_c)
        for i, buf in enumerate((tokb, cotb))
    ]

    gain, shift = gain_ref[...].reshape(1, WIDTH), shift_ref[...].reshape(1, WIDTH)

    def norm(rows):
        t = tokb[rows, :].astype(F32)
        t = t - jnp.mean(t, axis=-1, keepdims=True)
        inv = lax.rsqrt(jnp.mean(t * t, axis=-1, keepdims=True) + 1e-05)
        t = t * inv
        normed[rows, :] = (t * gain + shift).astype(BF)
        return t, inv

    t, inv = norm(own)
    xhat[...] = t
    rstd[...] = inv
    group, place = order_mask()
    row = lax.broadcasted_iota(jnp.int32, (128, WIDTH), 0)
    in_group = row == group
    hot = [(row == place + 2 * OWN * p).astype(F32) for p in range(4)]
    bias = jnp.zeros((128, 128), F32)
    for p in range(4):
        line = bin_ref[pl.ds(p * WIDTH, WIDTH)].reshape(1, WIDTH)
        bias = bias + dot_exact(hot[p], jnp.where(in_group, line, 0.0), ((1,), (1,)))
    for yy in range(NY):
        for xx in range(NX):
            g = group_of(xx, yy, 0)
            bcol[(yy * NX + xx) * CHUNK : (yy * NX + xx + 1) * CHUNK, :] = jnp.where(
                c == 0, bias[:CHUNK, g : g + 1], bias[:CHUNK, g + 1 : g + 2]
            )
    select = shard_select()
    for copy in cc:
        copy.wait_recv()
    norm(other)

    for copy in zc:
        copy.wait_recv()
    w = dot_nn(select, zbuf[...].reshape(NZ * SHARD, WIDTH)).astype(BF)
    win[y, x] = w[:CHUNK]
    wout[y, x] = w[CHUNK:]

    to = ((to_x[1], to_x[3]), (to_y[1], to_y[3]))

    class Item:
        def __init__(self, index, axis, slot, half):
            self.index, self.axis, self.half = index, axis, half
            self.at = [slot(d) for d in range(4)]
            self.copies = [None] * 4

        def go(self, k, ref):
            self.copies[k] = send(ref, ref, ws.at[self.index, k], wr.at[self.index, k], to[self.axis][k % 2])

        def start(self):
            self.go(0, self.at[0])
            self.go(1, self.at[0])

        def forward(self, k):
            self.copies[k].wait_recv()
            if k == 0:
                self.go(2, self.at[3].at[0 : self.half])
            else:
                self.go(3, self.at[1].at[self.half : CHUNK])

        def finish(self):
            self.copies[2].wait_recv()
            self.copies[3].wait_recv()

    first_in = Item(0, 0, lambda d: win.at[y, xp[d]], 48)
    first_out = Item(1, 1, lambda d: wout.at[yp[d], x], 48)
    later_in = [Item(2 + p, 1, lambda d, p=p: win.at[yp[d], xp[p]], (32, 48)[p % 2]) for p in range(4)]
    later_out = [Item(6 + p, 0, lambda d, p=p: wout.at[yp[p], xp[d]], (32, 48)[p % 2]) for p in range(4)]
    first_in.start()
    first_out.start()
    later_in[0].start()
    later_out[0].start()
    for k, p in ((0, 3), (1, 1)):
        first_in.forward(k)
        first_out.forward(k)
        later_in[p].start()
        later_out[p].start()
    for k in (0, 1):
        later_in[0].forward(k)
        later_out[0].forward(k)
    first_in.finish()
    first_out.finish()
    later_in[2].start()
    later_out[2].start()
    for p in (3, 1):
        for k in (0, 1):
            later_in[p].forward(k)
            later_out[p].forward(k)

    g1i, g1o = [], {}

    def block(d):
        by = yp[d]
        rows = pl.ds(pl.multiple_of(by * BLOCK, BLOCK), BLOCK)
        v = dot_nt(win[by].reshape(BLOCK, WIDTH), normed[...]) + bcol[rows, :]
        phi = 0.5 * (1.0 + lax.erf(v * 0.7071067811865476))
        slope = phi + v * jnp.exp(-0.5 * v * v) * 0.3989422804014327
        a = (v * phi).astype(BF)
        act[rows, :] = a
        dp = dot_nt(wout[by].reshape(BLOCK, WIDTH), cotb[...]) * slope
        folded = dp[:, 0:128]
        for j in range(1, 6):
            folded = folded + dp[:, 128 * j : 128 * j + 128]
        dbp[rows, :] = folded
        dp = dp.astype(BF)
        dpre[rows, :] = dp
        gin[by] = dot_nn(dp, normed[...]).astype(BF).reshape(NX, CHUNK, WIDTH)
        gout[by] = dot_nn(a, cotb[...]).astype(BF).reshape(NX, CHUNK, WIDTH)

    def block_send(d):
        by = yp[d]
        if d:
            g1i.append(send(gin.at[by], r1in.at[d - 1], g1is.at[d - 1], g1ir.at[d - 1], to_y[d]))
        g1o[d] = [
            send(gout.at[by, xp[e]], r1out.at[e - 1, by], g1os.at[d, e - 1], g1or.at[d, e - 1], to_x[e])
            for e in (2, 1, 3)
        ]

    later_out[0].finish()
    block(0)
    for k in (0, 1):
        later_in[2].forward(k)
        later_out[2].forward(k)
    block_send(0)
    for p in (1, 3):
        later_out[p].finish()
        block(p)
        block_send(p)
    later_out[2].finish()
    for p in range(4):
        later_in[p].finish()
    block(2)
    block_send(2)

    wi = win[...].reshape(HIDDEN, WIDTH)
    wo = wout[...].reshape(HIDDEN, WIDTH)
    pc = []
    part[0, 1] = dot_tn(act[:, other], wo)
    pc.append(send(part.at[0, 1], partr.at[0], ps.at[0], pr.at[0], to_c))
    part[1, 1] = dot_tn(dpre[:, other], wi)
    pc.append(send(part.at[1, 1], partr.at[1], ps.at[1], pr.at[1], to_c))
    part[0, 0] = dot_tn(act[:, own], wo)
    part[1, 0] = dot_tn(dpre[:, own], wi)
    cot = cotb[own, :].astype(F32)
    pc[0].wait_recv()
    layer = tokb[own, :].astype(F32) + (part[0, 0] + partr[0]) + bout_ref[...].reshape(1, WIDTH)
    layer_ref[0] = layer.astype(BF)[0:FRAMES]
    pc[1].wait_recv()
    dn = part[1, 0] + partr[1]
    xh = xhat[...]
    dx = dn * gain
    dt = cot + rstd[...] * (
        dx - jnp.mean(dx, axis=-1, keepdims=True) - xh * jnp.mean(dx * xh, axis=-1, keepdims=True)
    )
    dtok_ref[0] = dt.astype(BF)[0:FRAMES]

    lane = lax.broadcasted_iota(jnp.int32, (CHUNK, 128), 1)
    db = jnp.zeros((CHUNK, 128), F32)
    for yy in range(NY):
        for xx in range(NX):
            k = yy * NX + xx
            total = jnp.sum(dbp[k * CHUNK : (k + 1) * CHUNK, :], axis=1, keepdims=True)
            db = jnp.where(lane == group_of(xx, yy, c), total, db)
    for p in range(4):
        line = dot_exact(db, hot[p][:CHUNK], ((0,), (0,)))
        vown[p : p + 1, :] = jnp.sum(jnp.where(in_group, line, 0.0), axis=0, keepdims=True)
    vown[4:5, :] = jnp.sum(dn * xh, axis=0, keepdims=True)
    vown[5:6, :] = jnp.sum(dn, axis=0, keepdims=True)
    vown[6:7, :] = jnp.sum(cot, axis=0, keepdims=True)
    vown[7:8, :] = jnp.zeros((1, WIDTH), F32)
    vc = send(vown, vcore, vs.at[0], vr.at[0], to_c)
    vc.wait_recv()
    vy[y] = vown[...] + vcore[...]
    vyc = [send(vy.at[y], vy.at[y], vs.at[d], vr.at[d], to_y[d]) for d in (1, 3, 2)]

    g2 = []

    def add_in():
        for copy in g1i:
            copy.wait_recv()
        for d in (1, 3, 2, 0):
            q = xp[d]
            total = gin[y, q].astype(F32)
            for e in range(3):
                total = total + r1in[e, q].astype(F32)
            s1in[q] = total.astype(BF)
            if d:
                g2.append(send(s1in.at[q], r2in.at[d - 1], g2s.at[0, d - 1], g2r.at[0, d - 1], to_x[d]))

    def add_out(d):
        for copy in g1o[d]:
            copy.wait_recv()
        q = yp[d]
        total = gout[q, x].astype(F32)
        for e in range(3):
            total = total + r1out[e, q].astype(F32)
        s1out[q] = total.astype(BF)
        if d:
            g2.append(send(s1out.at[q], r2out.at[d - 1], g2s.at[1, d - 1], g2r.at[1, d - 1], to_y[d]))

    for d in (0, 1, 3, 2):
        add_out(d)
    add_in()
    for copy in vyc:
        copy.wait_recv()
    vx[x] = (vy[0] + vy[1]) + (vy[2] + vy[3])
    vxc = [send(vx.at[x], vx.at[x], vs.at[3 + d], vr.at[3 + d], to_x[d]) for d in (1, 3, 2)]

    for copy in g2:
        copy.wait_recv()
    sums = []
    for first, got in ((s1in[x], r2in), (s1out[y], r2out)):
        total = first.astype(F32)
        for d in range(3):
            total = total + got[d].astype(F32)
        sums.append(total.astype(BF))
    both = jnp.concatenate(sums, axis=0)
    zsend[...] = dot_tn(select, both).astype(BF).reshape(NZ, SHARD, WIDTH)
    g3 = [
        send(zsend.at[zp[d]], r3.at[d - 1], g3s.at[d - 1], g3r.at[d - 1], to_z[d])
        for d in (4, 3, 5, 2, 6, 1, 7)
    ]
    for copy in vxc:
        copy.wait_recv()
    vz[z] = (vx[0] + vx[1]) + (vx[2] + vx[3])
    vzc = [send(vz.at[z], vz.at[z], vs.at[6 + d], vr.at[6 + d], to_z[d]) for d in (4, 3, 5, 2, 6, 1, 7)]

    for copy in g3:
        copy.wait_recv()
    grad = zsend[z].astype(F32)
    for d in range(NZ - 1):
        grad = grad + r3[d].astype(F32)
    grad = grad * (1.0 / math.sqrt(TOKENS))
    grad_ref[...] = grad
    for copy in vzc:
        copy.wait_recv()
    total = vz[0]
    for q in range(1, NZ):
        total = total + vz[q]
    vec_ref[...] = total * (1.0 / math.sqrt(TOKENS))
    for copy in pending:
        copy.wait_send()


def update_kernel(
    layer_ref, dtok_ref, vec_ref, grad_ref,
    min_ref, vin_ref, qin_ref, mout_ref, vout_ref, qout_ref,
    olayer_ref, odtok_ref, ogain_ref, oshift_ref, obin_ref, obout_ref,
    omin_ref, ovin_ref, oqin_ref, omout_ref, ovout_ref, oqout_ref,
):
    olayer_ref[...] = layer_ref[...]
    odtok_ref[...] = dtok_ref[...]
    omin_ref[...], ovin_ref[...], oqin_ref[...] = adamw(
        min_ref[...], vin_ref[...], qin_ref[...], grad_ref[0:OWN, :]
    )
    omout_ref[...], ovout_ref[...], oqout_ref[...] = adamw(
        mout_ref[...], vout_ref[...], qout_ref[...], grad_ref[16 : 16 + OWN, :]
    )
    for p in range(4):
        obin_ref[pl.ds(p * WIDTH, WIDTH)] = vec_ref[p : p + 1, :].reshape(WIDTH)
    ogain_ref[...] = vec_ref[4:5, :].reshape(WIDTH)
    oshift_ref[...] = vec_ref[5:6, :].reshape(WIDTH)
    obout_ref[...] = vec_ref[6:7, :].reshape(WIDTH)


def body(
    tokens, cotangent, codes_in, scales_in, codes_out, scales_out,
    layer_norm_gain, layer_norm_bias, bias_in, bias_out,
    master_in, moment_in, second_in, master_out, moment_out, second_out,
):
    vmem = pl.BlockSpec(memory_space=pltpu.VMEM)
    owned = jax.ShapeDtypeStruct((OWN, WIDTH), F32)
    dma = pltpu.SemaphoreType.DMA
    layer, d_tokens, vec, grad = pl.pallas_call(
        kernel,
        out_shape=[
            jax.ShapeDtypeStruct(tokens.shape, BF),
            jax.ShapeDtypeStruct(tokens.shape, BF),
            jax.ShapeDtypeStruct((8, WIDTH), F32),
            jax.ShapeDtypeStruct((SHARD, WIDTH), F32),
        ],
        in_specs=[vmem] * 10,
        out_specs=[vmem] * 4,
        scratch_shapes=[
            pltpu.VMEM((2 * ROWS, WIDTH), BF),
            pltpu.VMEM((2 * ROWS, WIDTH), BF),
            pltpu.VMEM((2 * ROWS, WIDTH), BF),
            pltpu.VMEM((ROWS, WIDTH), F32),
            pltpu.VMEM((ROWS, 1), F32),
            pltpu.VMEM((SHARD, WIDTH), BF),
            pltpu.VMEM((NZ, SHARD, WIDTH), BF),
            pltpu.VMEM((NY, NX, CHUNK, WIDTH), BF),
            pltpu.VMEM((NY, NX, CHUNK, WIDTH), BF),
            pltpu.VMEM((HIDDEN, 1), F32),
            pltpu.VMEM((HIDDEN, 128), F32),
            pltpu.VMEM((HIDDEN, 2 * ROWS), BF),
            pltpu.VMEM((HIDDEN, 2 * ROWS), BF),
            pltpu.VMEM((NY, NX, CHUNK, WIDTH), BF),
            pltpu.VMEM((NY, NX, CHUNK, WIDTH), BF),
            pltpu.VMEM((NY - 1, NX, CHUNK, WIDTH), BF),
            pltpu.VMEM((NX - 1, NY, CHUNK, WIDTH), BF),
            pltpu.VMEM((NX, CHUNK, WIDTH), BF),
            pltpu.VMEM((NY, CHUNK, WIDTH), BF),
            pltpu.VMEM((NX - 1, CHUNK, WIDTH), BF),
            pltpu.VMEM((NY - 1, CHUNK, WIDTH), BF),
            pltpu.VMEM((NZ, SHARD, WIDTH), BF),
            pltpu.VMEM((NZ - 1, SHARD, WIDTH), BF),
            pltpu.VMEM((2, 2, ROWS, WIDTH), F32),
            pltpu.VMEM((2, ROWS, WIDTH), F32),
            pltpu.VMEM((8, WIDTH), F32),
            pltpu.VMEM((8, WIDTH), F32),
            pltpu.VMEM((NY, 8, WIDTH), F32),
            pltpu.VMEM((NX, 8, WIDTH), F32),
            pltpu.VMEM((NZ, 8, WIDTH), F32),
            dma((2,)), dma((2,)),
            dma((7,)), dma((7,)),
            dma((10, 4)), dma((10, 4)),
            dma((3,)), dma((3,)),
            dma((4, 3)), dma((4, 3)),
            dma((2, 3)), dma((2, 3)),
            dma((7,)), dma((7,)),
            dma((2,)), dma((2,)),
            dma((14,)), dma((14,)),
        ],
        compiler_params=pltpu.CompilerParams(
            collective_id=0, has_side_effects=True, vmem_limit_bytes=56 * 2**20
        ),
    )(
        tokens, cotangent, codes_in, scales_in, codes_out, scales_out,
        layer_norm_gain, layer_norm_bias, bias_in, bias_out,
    )
    return tuple(
        pl.pallas_call(
            update_kernel,
            out_shape=[jax.ShapeDtypeStruct(tokens.shape, BF)] * 2
            + [jax.ShapeDtypeStruct((n,), F32) for n in (WIDTH, WIDTH, NC * HIDDEN, WIDTH)]
            + [owned] * 6,
            in_specs=[vmem] * 10,
            out_specs=[vmem] * 12,
            compiler_params=pltpu.CompilerParams(vmem_limit_bytes=32 * 2**20),
        )(
            layer, d_tokens, vec, grad,
            master_in, moment_in, second_in, master_out, moment_out, second_out,
        )
    )


def solution(mesh):
    tokens, rows, whole = P("fsdp", "seq", None), P(("fsdp", "seq"), None), P()
    return jax.shard_map(
        body,
        mesh=mesh,
        in_specs=(tokens,) * 2 + (rows,) * 4 + (whole,) * 4 + (rows,) * 6,
        out_specs=(tokens,) * 2 + (whole,) * 4 + (rows,) * 6,
        check_vma=False,
    )
```

```python
import math

import jax
import jax.numpy as jnp
from jax import lax
from jax.experimental import pallas as pl
from jax.experimental.pallas import tpu as pltpu
from jax.sharding import PartitionSpec as P

NX, NY, NZ, NC = 4, 4, 8, 2
WIDTH = 640
OWN = 10
FRAMES = 375
ROWS = 384
CHUNK = NZ * OWN
BLOCK = NX * CHUNK
HIDDEN = NY * BLOCK
PACK = 112
SHARD = 32
TOKENS = 96000
BF, F32 = jnp.bfloat16, jnp.float32
MESH = pl.DeviceIdType.MESH


def dot_nn(a, b):
    return jnp.dot(a, b, preferred_element_type=F32)


def dot_nt(a, b):
    return lax.dot_general(a, b, (((1,), (1,)), ((), ())), preferred_element_type=F32)


def dot_tn(a, b):
    return lax.dot_general(a, b, (((0,), (0,)), ((), ())), preferred_element_type=F32)


def coordinates():
    f = lax.axis_index("fsdp")
    s = lax.axis_index("seq")
    y = lax.rem(f, 4)
    x_hi = lax.rem(f // 4, 2)
    return x_hi * 2 + s // 2, y, f // 8, lax.rem(s, 2)


def device(x, y, z, c):
    return ((z * 2 + x // 2) * 4 + y, lax.rem(x, 2) * 2 + c)


def decode(codes, scales):
    spread = (
        lax.broadcasted_iota(jnp.int32, (20, WIDTH), 1) // 32
        == lax.broadcasted_iota(jnp.int32, (20, WIDTH), 0)
    )
    k = dot_nn((scales - 118).astype(F32).astype(BF), spread.astype(F32).astype(BF)).astype(jnp.int32)
    negative = codes >= 128
    e = (codes >> 3) & 15
    m = codes & 7
    whole = jnp.where(e > 0, m + 8, m)
    value = (whole << (jnp.maximum(e, 1) + k - 1)).astype(F32) * (2.0**-18)
    return jnp.where(negative, -value, value)


def shard_pack(shard_ref):
    r = lax.broadcasted_iota(jnp.int32, (PACK, SHARD), 0)
    col = lax.broadcasted_iota(jnp.int32, (PACK, SHARD), 1)
    col = jnp.where(col < 16, jnp.where(col < OWN, col, -PACK), jnp.where(col < 16 + OWN, col - 6, -PACK))
    out = jnp.zeros((PACK, 128), F32)
    for j in range(5):
        hot = (r - 2 * OWN * j == col).astype(F32).astype(BF)
        out = out + dot_nn(hot, shard_ref[:, 128 * j : 128 * j + 128])
    return out.astype(BF)


def fill_select(sel_ref):
    r = lax.broadcasted_iota(jnp.int32, (2 * CHUNK, NZ * PACK), 0)
    col = lax.broadcasted_iota(jnp.int32, (2 * CHUNK, NZ * PACK), 1)
    second = (r >= CHUNK).astype(jnp.int32)
    r = r - CHUNK * second
    z = jnp.zeros_like(r)
    for j in range(1, NZ):
        z = z + (r >= OWN * j).astype(jnp.int32)
    gap = col - (z * (PACK - OWN) + r + OWN * second)
    for j in range(5):
        sel_ref[j] = (gap == 2 * OWN * j).astype(F32).astype(BF)


def order_mask():
    j = lax.broadcasted_iota(jnp.int32, (128, WIDTH), 1)
    later = (j >= 320).astype(jnp.int32)
    j = j - 320 * later
    group = (j * 6554) >> 16
    return group, later * OWN + j - OWN * group


def group_of(xx, yy, c):
    return ((xx // 2 * 4 + yy) * 2 + xx % 2) * 2 + c


def dot_exact(a, b, dims):
    return lax.dot_general(
        a, b, (dims, ((), ())), preferred_element_type=F32, precision=lax.Precision.HIGHEST
    )


def adamw(master, moment, second, grad):
    new_moment = 0.9 * moment + 0.1 * grad
    new_second = 0.95 * second + 0.05 * grad * grad
    new_master = master - 0.001 * (new_moment / (jnp.sqrt(new_second) + 1e-08) + 0.1 * master)
    return new_master, new_moment, new_second


def kernel(
    tok_ref, cot_ref, cin_ref, sin_ref, cout_ref, sout_ref,
    gain_ref, shift_ref, bin_ref, bout_ref,
    layer_ref, dtok_ref, ogain_ref, oshift_ref, obin_ref, obout_ref, gradin_ref, gradout_ref,
    tokv, cotv, layv, dtv, sel, tokb, cotb, normed, xhat, rstd, shard, zpk, zbuf, win, wout, bcol, dbp, act, dpre,
    gin, gout, r1in, r1out, s1in, s1out, r2in, r2out, zsend, r3,
    part, partr, vown, vcore, vy, vx, vz,
    cs, cr, zs, zr, ws, wr, g1is, g1ir, g1os, g1or, g2s, g2r, g3s, g3r, ps, pr, vs, vr, ls,
):
    x, y, z, c = coordinates()
    xp = [lax.rem(x + d, NX) for d in range(NX)]
    yp = [lax.rem(y + d, NY) for d in range(NY)]
    zp = [lax.rem(z + d, NZ) for d in range(NZ)]
    to_x = [device(q, y, z, c) for q in xp]
    to_y = [device(x, q, z, c) for q in yp]
    to_z = [device(x, y, q, c) for q in zp]
    to_c = device(x, y, z, 1 - c)
    pending = []

    def send(src, dst, ssem, rsem, target):
        copy = pltpu.make_async_remote_copy(
            src_ref=src, dst_ref=dst, send_sem=ssem, recv_sem=rsem,
            device_id=target, device_id_type=MESH,
        )
        copy.start()
        pending.append(copy)
        return copy

    barrier = pltpu.get_barrier_semaphore()
    for q in to_x[1:] + to_y[1:] + to_z[1:] + [to_c]:
        pl.semaphore_signal(barrier, inc=1, device_id=q, device_id_type=MESH)

    loads = [
        pltpu.make_async_copy(tok_ref, tokv, ls.at[0]),
        pltpu.make_async_copy(cot_ref, cotv, ls.at[1]),
    ]
    for copy in loads:
        copy.start()
    shard[...] = jnp.zeros_like(shard)
    shard[0:OWN, :] = decode(cin_ref[...], sin_ref[...]).astype(BF)
    shard[16 : 16 + OWN, :] = decode(cout_ref[...], sout_ref[...]).astype(BF)
    zpk[...] = shard_pack(shard)
    zbuf[z] = zpk[...]
    pl.semaphore_wait(barrier, NX + NY + NZ - 2)

    zc = [
        send(zpk, zbuf.at[z], zs.at[d - 1], zr.at[d - 1], to_z[d])
        for d in (4, 3, 5, 2, 6, 1, 7)
    ]
    for copy, buf, ref in zip(loads, (tokb, cotb), (tokv, cotv)):
        copy.wait()
        buf[ROWS - 16 : ROWS, :] = jnp.zeros((16, WIDTH), BF)
        buf[0:FRAMES, :] = ref[0]
    own, other = slice(0, ROWS), slice(ROWS, 2 * ROWS)
    cc = [
        send(buf.at[own], buf.at[other], cs.at[i], cr.at[i], to_c)
        for i, buf in enumerate((tokb, cotb))
    ]

    gain, shift = gain_ref[...].reshape(1, WIDTH), shift_ref[...].reshape(1, WIDTH)

    def norm(rows):
        t = tokb[rows, :].astype(F32)
        t = t - jnp.mean(t, axis=-1, keepdims=True)
        inv = lax.rsqrt(jnp.mean(t * t, axis=-1, keepdims=True) + 1e-05)
        t = t * inv
        normed[rows, :] = (t * gain + shift).astype(BF)
        return t, inv

    t, inv = norm(own)
    xhat[...] = t
    rstd[...] = inv
    group, place = order_mask()
    row = lax.broadcasted_iota(jnp.int32, (128, WIDTH), 0)
    in_group = row == group
    hot = [(row == place + 2 * OWN * p).astype(F32) for p in range(4)]
    bias = jnp.zeros((128, 128), F32)
    for p in range(4):
        line = bin_ref[pl.ds(p * WIDTH, WIDTH)].reshape(1, WIDTH)
        bias = bias + dot_exact(hot[p], jnp.where(in_group, line, 0.0), ((1,), (1,)))
    for yy in range(NY):
        for xx in range(NX):
            g = group_of(xx, yy, 0)
            bcol[(yy * NX + xx) * CHUNK : (yy * NX + xx + 1) * CHUNK, :] = jnp.where(
                c == 0, bias[:CHUNK, g : g + 1], bias[:CHUNK, g + 1 : g + 2]
            )
    fill_select(sel)
    for copy in cc:
        copy.wait_recv()
    norm(other)

    for copy in zc:
        copy.wait_recv()
    lines = zbuf[...].reshape(NZ * PACK, 128)
    for j in range(5):
        w = dot_nn(sel[j], lines).astype(BF)
        win[y, x, :, 128 * j : 128 * j + 128] = w[:CHUNK]
        wout[y, x, :, 128 * j : 128 * j + 128] = w[CHUNK:]

    to = ((to_x[1], to_x[3]), (to_y[1], to_y[3]))

    class Item:
        def __init__(self, index, axis, slot, half):
            self.index, self.axis, self.half = index, axis, half
            self.at = [slot(d) for d in range(4)]
            self.copies = [None] * 4

        def go(self, k, ref):
            self.copies[k] = send(ref, ref, ws.at[self.index, k], wr.at[self.index, k], to[self.axis][k % 2])

        def start(self):
            self.go(0, self.at[0])
            self.go(1, self.at[0])

        def forward(self, k):
            self.copies[k].wait_recv()
            if k == 0:
                self.go(2, self.at[3].at[0 : self.half])
            else:
                self.go(3, self.at[1].at[self.half : CHUNK])

        def finish(self):
            self.copies[2].wait_recv()
            self.copies[3].wait_recv()

    first_in = Item(0, 0, lambda d: win.at[y, xp[d]], 48)
    first_out = Item(1, 1, lambda d: wout.at[yp[d], x], 48)
    later_in = [Item(2 + p, 1, lambda d, p=p: win.at[yp[d], xp[p]], (32, 48)[p % 2]) for p in range(4)]
    later_out = [Item(6 + p, 0, lambda d, p=p: wout.at[yp[p], xp[d]], (32, 48)[p % 2]) for p in range(4)]
    first_in.start()
    first_out.start()
    later_in[0].start()
    later_out[0].start()
    for k, p in ((0, 3), (1, 1)):
        first_in.forward(k)
        first_out.forward(k)
        later_in[p].start()
        later_out[p].start()
    for k in (0, 1):
        later_in[0].forward(k)
        later_out[0].forward(k)
    first_in.finish()
    first_out.finish()
    later_in[2].start()
    later_out[2].start()
    for p in (3, 1):
        for k in (0, 1):
            later_in[p].forward(k)
            later_out[p].forward(k)

    g1i, g1o = [], {}

    def block(d):
        by = yp[d]
        rows = pl.ds(pl.multiple_of(by * BLOCK, BLOCK), BLOCK)
        v = dot_nt(win[by].reshape(BLOCK, WIDTH), normed[...]) + bcol[rows, :]
        phi = 0.5 * (1.0 + lax.erf(v * 0.7071067811865476))
        slope = phi + v * jnp.exp(-0.5 * v * v) * 0.3989422804014327
        a = (v * phi).astype(BF)
        act[rows, :] = a
        dp = dot_nt(wout[by].reshape(BLOCK, WIDTH), cotb[...]) * slope
        folded = dp[:, 0:128]
        for j in range(1, 6):
            folded = folded + dp[:, 128 * j : 128 * j + 128]
        dbp[rows, :] = folded
        dp = dp.astype(BF)
        dpre[rows, :] = dp
        gin[by] = dot_nn(dp, normed[...]).astype(BF).reshape(NX, CHUNK, WIDTH)
        gout[by] = dot_nn(a, cotb[...]).astype(BF).reshape(NX, CHUNK, WIDTH)

    def block_send(d):
        by = yp[d]
        if d:
            g1i.append(send(gin.at[by], r1in.at[d - 1], g1is.at[d - 1], g1ir.at[d - 1], to_y[d]))
        g1o[d] = [
            send(gout.at[by, xp[e]], r1out.at[e - 1, by], g1os.at[d, e - 1], g1or.at[d, e - 1], to_x[e])
            for e in (2, 1, 3)
        ]

    later_out[0].finish()
    block(0)
    for k in (0, 1):
        later_in[2].forward(k)
        later_out[2].forward(k)
    block_send(0)
    for p in (1, 3):
        later_out[p].finish()
        block(p)
        block_send(p)
    later_out[2].finish()
    for p in range(4):
        later_in[p].finish()
    block(2)
    block_send(2)

    wi = win[...].reshape(HIDDEN, WIDTH)
    wo = wout[...].reshape(HIDDEN, WIDTH)
    pc = []
    part[0, 1] = dot_tn(act[:, other], wo)
    pc.append(send(part.at[0, 1], partr.at[0], ps.at[0], pr.at[0], to_c))
    part[1, 1] = dot_tn(dpre[:, other], wi)
    pc.append(send(part.at[1, 1], partr.at[1], ps.at[1], pr.at[1], to_c))
    part[0, 0] = dot_tn(act[:, own], wo)
    part[1, 0] = dot_tn(dpre[:, own], wi)
    cot = cotb[own, :].astype(F32)
    pc[0].wait_recv()
    layer = tokb[own, :].astype(F32) + (part[0, 0] + partr[0]) + bout_ref[...].reshape(1, WIDTH)
    layv[0] = layer.astype(BF)[0:FRAMES]
    stores = [
        pltpu.make_async_copy(layv, layer_ref, ls.at[2]),
        pltpu.make_async_copy(dtv, dtok_ref, ls.at[3]),
    ]
    stores[0].start()
    pc[1].wait_recv()
    dn = part[1, 0] + partr[1]
    xh = xhat[...]
    dx = dn * gain
    dt = cot + rstd[...] * (
        dx - jnp.mean(dx, axis=-1, keepdims=True) - xh * jnp.mean(dx * xh, axis=-1, keepdims=True)
    )
    dtv[0] = dt.astype(BF)[0:FRAMES]
    stores[1].start()

    lane = lax.broadcasted_iota(jnp.int32, (CHUNK, 128), 1)
    db = jnp.zeros((CHUNK, 128), F32)
    for yy in range(NY):
        for xx in range(NX):
            k = yy * NX + xx
            total = jnp.sum(dbp[k * CHUNK : (k + 1) * CHUNK, :], axis=1, keepdims=True)
            db = jnp.where(lane == group_of(xx, yy, c), total, db)
    for p in range(4):
        line = dot_exact(db, hot[p][:CHUNK], ((0,), (0,)))
        vown[p : p + 1, :] = jnp.sum(jnp.where(in_group, line, 0.0), axis=0, keepdims=True)
    vown[4:5, :] = jnp.sum(dn * xh, axis=0, keepdims=True)
    vown[5:6, :] = jnp.sum(dn, axis=0, keepdims=True)
    vown[6:7, :] = jnp.sum(cot, axis=0, keepdims=True)
    vown[7:8, :] = jnp.zeros((1, WIDTH), F32)
    vc = send(vown, vcore, vs.at[0], vr.at[0], to_c)
    vc.wait_recv()
    vz[z] = vown[...] + vcore[...]
    vzc = [send(vz.at[z], vz.at[z], vs.at[6 + d], vr.at[6 + d], to_z[d]) for d in (4, 3, 5, 2, 6, 1, 7)]

    g2 = []

    def add_in():
        for copy in g1i:
            copy.wait_recv()
        for d in (1, 3, 2, 0):
            q = xp[d]
            total = gin[y, q].astype(F32)
            for e in range(3):
                total = total + r1in[e, q].astype(F32)
            s1in[q] = total.astype(BF)
            if d:
                g2.append(send(s1in.at[q], r2in.at[d - 1], g2s.at[0, d - 1], g2r.at[0, d - 1], to_x[d]))

    def add_out(d):
        for copy in g1o[d]:
            copy.wait_recv()
        q = yp[d]
        total = gout[q, x].astype(F32)
        for e in range(3):
            total = total + r1out[e, q].astype(F32)
        s1out[q] = total.astype(BF)
        if d:
            g2.append(send(s1out.at[q], r2out.at[d - 1], g2s.at[1, d - 1], g2r.at[1, d - 1], to_y[d]))

    for d in (0, 1, 3):
        add_out(d)
    for copy in vzc:
        copy.wait_recv()
    total = vz[0]
    for q in range(1, NZ):
        total = total + vz[q]
    vy[y] = total
    vyc = [send(vy.at[y], vy.at[y], vs.at[d], vr.at[d], to_y[d]) for d in (1, 3, 2)]
    add_in()
    add_out(2)
    for copy in vyc:
        copy.wait_recv()
    vx[x] = (vy[0] + vy[1]) + (vy[2] + vy[3])
    vxc = [send(vx.at[x], vx.at[x], vs.at[3 + d], vr.at[3 + d], to_x[d]) for d in (1, 3, 2)]

    for copy in g2:
        copy.wait_recv()
    sums = []
    for first, got in ((s1in[x], r2in), (s1out[y], r2out)):
        total = first.astype(F32)
        for d in range(3):
            total = total + got[d].astype(F32)
        sums.append(total.astype(BF))
    both = jnp.concatenate(sums, axis=0)
    packed = jnp.zeros((NZ * PACK, 128), F32)
    for j in range(5):
        packed = packed + dot_tn(sel[j], both[:, 128 * j : 128 * j + 128])
    zsend[...] = packed.astype(BF).reshape(NZ, PACK, 128)
    g3 = [
        send(zsend.at[zp[d]], r3.at[d - 1], g3s.at[d - 1], g3r.at[d - 1], to_z[d])
        for d in (4, 3, 5, 2, 6, 1, 7)
    ]

    for copy in vxc:
        copy.wait_recv()
    total = (vx[0] + vx[1]) + (vx[2] + vx[3])
    for p in range(4):
        obin_ref[pl.ds(p * WIDTH, WIDTH)] = total[p : p + 1].reshape(WIDTH)
    ogain_ref[...] = total[4:5].reshape(WIDTH)
    oshift_ref[...] = total[5:6].reshape(WIDTH)
    obout_ref[...] = total[6:7].reshape(WIDTH)

    for copy in g3:
        copy.wait_recv()
    grad = zsend[z].astype(F32)
    for d in range(NZ - 1):
        grad = grad + r3[d].astype(F32)
    for j in range(5):
        cols = slice(128 * j, 128 * j + 128)
        gradin_ref[:, cols] = grad[2 * OWN * j : 2 * OWN * j + OWN]
        gradout_ref[:, cols] = grad[2 * OWN * j + OWN : 2 * OWN * (j + 1)]
    for copy in stores:
        copy.wait()
    for copy in pending:
        copy.wait_send()


def body(
    tokens, cotangent, codes_in, scales_in, codes_out, scales_out,
    layer_norm_gain, layer_norm_bias, bias_in, bias_out,
    master_in, moment_in, second_in, master_out, moment_out, second_out,
):
    vmem = pl.BlockSpec(memory_space=pltpu.VMEM)
    owned = jax.ShapeDtypeStruct((OWN, WIDTH), F32)
    dma = pltpu.SemaphoreType.DMA
    hbm = pl.BlockSpec(memory_space=pl.ANY)
    rounded = pltpu.VMEM(tokens.shape, BF)
    outs = pl.pallas_call(
        kernel,
        out_shape=[jax.ShapeDtypeStruct(tokens.shape, BF)] * 2
        + [jax.ShapeDtypeStruct((n,), F32) for n in (WIDTH, WIDTH, NC * HIDDEN, WIDTH)]
        + [owned] * 2,
        in_specs=[hbm] * 2 + [vmem] * 8,
        out_specs=[hbm] * 2 + [vmem] * 6,
        scratch_shapes=[rounded] * 4
        + [
            pltpu.VMEM((5, 2 * CHUNK, NZ * PACK), BF),
            pltpu.VMEM((2 * ROWS, WIDTH), BF),
            pltpu.VMEM((2 * ROWS, WIDTH), BF),
            pltpu.VMEM((2 * ROWS, WIDTH), BF),
            pltpu.VMEM((ROWS, WIDTH), F32),
            pltpu.VMEM((ROWS, 1), F32),
            pltpu.VMEM((SHARD, WIDTH), BF),
            pltpu.VMEM((PACK, 128), BF),
            pltpu.VMEM((NZ, PACK, 128), BF),
            pltpu.VMEM((NY, NX, CHUNK, WIDTH), BF),
            pltpu.VMEM((NY, NX, CHUNK, WIDTH), BF),
            pltpu.VMEM((HIDDEN, 1), F32),
            pltpu.VMEM((HIDDEN, 128), F32),
            pltpu.VMEM((HIDDEN, 2 * ROWS), BF),
            pltpu.VMEM((HIDDEN, 2 * ROWS), BF),
            pltpu.VMEM((NY, NX, CHUNK, WIDTH), BF),
            pltpu.VMEM((NY, NX, CHUNK, WIDTH), BF),
            pltpu.VMEM((NY - 1, NX, CHUNK, WIDTH), BF),
            pltpu.VMEM((NX - 1, NY, CHUNK, WIDTH), BF),
            pltpu.VMEM((NX, CHUNK, WIDTH), BF),
            pltpu.VMEM((NY, CHUNK, WIDTH), BF),
            pltpu.VMEM((NX - 1, CHUNK, WIDTH), BF),
            pltpu.VMEM((NY - 1, CHUNK, WIDTH), BF),
            pltpu.VMEM((NZ, PACK, 128), BF),
            pltpu.VMEM((NZ - 1, PACK, 128), BF),
            pltpu.VMEM((2, 2, ROWS, WIDTH), F32),
            pltpu.VMEM((2, ROWS, WIDTH), F32),
            pltpu.VMEM((8, WIDTH), F32),
            pltpu.VMEM((8, WIDTH), F32),
            pltpu.VMEM((NY, 8, WIDTH), F32),
            pltpu.VMEM((NX, 8, WIDTH), F32),
            pltpu.VMEM((NZ, 8, WIDTH), F32),
            dma((2,)), dma((2,)),
            dma((7,)), dma((7,)),
            dma((10, 4)), dma((10, 4)),
            dma((3,)), dma((3,)),
            dma((4, 3)), dma((4, 3)),
            dma((2, 3)), dma((2, 3)),
            dma((7,)), dma((7,)),
            dma((2,)), dma((2,)),
            dma((14,)), dma((14,)),
            dma((4,)),
        ],
        compiler_params=pltpu.CompilerParams(
            collective_id=0, has_side_effects=True, vmem_limit_bytes=56 * 2**20
        ),
    )(
        tokens, cotangent, codes_in, scales_in, codes_out, scales_out,
        layer_norm_gain, layer_norm_bias, bias_in, bias_out,
    )
    sums = [total * (1.0 / math.sqrt(TOKENS)) for total in outs[2:]]
    return (
        tuple(outs[:2])
        + tuple(sums[:4])
        + adamw(master_in, moment_in, second_in, sums[4])
        + adamw(master_out, moment_out, second_out, sums[5])
    )


def solution(mesh):
    tokens, rows, whole = P("fsdp", "seq", None), P(("fsdp", "seq"), None), P()
    return jax.shard_map(
        body,
        mesh=mesh,
        in_specs=(tokens,) * 2 + (rows,) * 4 + (whole,) * 4 + (rows,) * 6,
        out_specs=(tokens,) * 2 + (whole,) * 4 + (rows,) * 6,
        check_vma=False,
    )
```

```python
import math

import jax
import jax.numpy as jnp
from jax import lax
from jax.experimental import pallas as pl
from jax.experimental.pallas import tpu as pltpu
from jax.sharding import PartitionSpec as P

NX, NY, NZ, NC = 4, 4, 8, 2
WIDTH = 640
OWN = 10
FRAMES = 375
ROWS = 384
CHUNK = NZ * OWN
BLOCK = NX * CHUNK
HIDDEN = NY * BLOCK
PACK = 112
PLACE = (0, 20, 40, 64, 84)
PARTS = ((slice(0, 384), slice(0, 64), (0, 1, 2)), (slice(384, 640), slice(64, 112), (3, 4)))
SHARD = 32
TOKENS = 96000
BF, F32 = jnp.bfloat16, jnp.float32
MESH = pl.DeviceIdType.MESH


def dot_nn(a, b):
    return jnp.dot(a, b, preferred_element_type=F32)


def dot_nt(a, b):
    return lax.dot_general(a, b, (((1,), (1,)), ((), ())), preferred_element_type=F32)


def dot_tn(a, b):
    return lax.dot_general(a, b, (((0,), (0,)), ((), ())), preferred_element_type=F32)


def coordinates():
    f = lax.axis_index("fsdp")
    s = lax.axis_index("seq")
    y = lax.rem(f, 4)
    x_hi = lax.rem(f // 4, 2)
    return x_hi * 2 + s // 2, y, f // 8, lax.rem(s, 2)


def device(x, y, z, c):
    return ((z * 2 + x // 2) * 4 + y, lax.rem(x, 2) * 2 + c)


def decode(codes, scales):
    spread = (
        lax.broadcasted_iota(jnp.int32, (20, WIDTH), 1) // 32
        == lax.broadcasted_iota(jnp.int32, (20, WIDTH), 0)
    )
    k = dot_nn((scales - 118).astype(F32).astype(BF), spread.astype(F32).astype(BF)).astype(jnp.int32)
    negative = codes >= 128
    e = (codes >> 3) & 15
    m = codes & 7
    whole = jnp.where(e > 0, m + 8, m)
    value = (whole << (jnp.maximum(e, 1) + k - 1)).astype(F32) * (2.0**-18)
    return jnp.where(negative, -value, value)


def shard_pack(shard_ref):
    r = lax.broadcasted_iota(jnp.int32, (PACK, SHARD), 0)
    col = lax.broadcasted_iota(jnp.int32, (PACK, SHARD), 1)
    col = jnp.where(col < 16, jnp.where(col < OWN, col, -PACK), jnp.where(col < 16 + OWN, col - 6, -PACK))
    out = jnp.zeros((PACK, 128), F32)
    for j in range(5):
        hot = (r - PLACE[j] == col).astype(F32).astype(BF)
        out = out + dot_nn(hot, shard_ref[:, 128 * j : 128 * j + 128])
    return out.astype(BF)


def fill_select(sel_ref):
    r = lax.broadcasted_iota(jnp.int32, (2 * CHUNK, NZ * PACK), 0)
    col = lax.broadcasted_iota(jnp.int32, (2 * CHUNK, NZ * PACK), 1)
    second = (r >= CHUNK).astype(jnp.int32)
    r = r - CHUNK * second
    z = jnp.zeros_like(r)
    for j in range(1, NZ):
        z = z + (r >= OWN * j).astype(jnp.int32)
    gap = col - (z * (PACK - OWN) + r + OWN * second)
    for j in range(5):
        sel_ref[j] = (gap == PLACE[j]).astype(F32).astype(BF)


def order_mask():
    j = lax.broadcasted_iota(jnp.int32, (128, WIDTH), 1)
    later = (j >= 320).astype(jnp.int32)
    j = j - 320 * later
    group = (j * 6554) >> 16
    return group, later * OWN + j - OWN * group


def group_of(xx, yy, c):
    return ((xx // 2 * 4 + yy) * 2 + xx % 2) * 2 + c


def dot_exact(a, b, dims):
    return lax.dot_general(
        a, b, (dims, ((), ())), preferred_element_type=F32, precision=lax.Precision.HIGHEST
    )


def adamw(master, moment, second, grad):
    new_moment = 0.9 * moment + 0.1 * grad
    new_second = 0.95 * second + 0.05 * grad * grad
    new_master = master - 0.001 * (new_moment / (jnp.sqrt(new_second) + 1e-08) + 0.1 * master)
    return new_master, new_moment, new_second


def kernel(
    tok_ref, cot_ref, cin_ref, sin_ref, cout_ref, sout_ref,
    gain_ref, shift_ref, bin_ref, bout_ref,
    layer_ref, dtok_ref, ogain_ref, oshift_ref, obin_ref, obout_ref, gradin_ref, gradout_ref,
    tokv, cotv, layv, dtv, sel, tokb, cotb, normed, xhat, rstd, shard, zpk, zbuf, win, wout, bcol, dbp, act, dpre,
    gin, gout, r1in, r1out, s1in, s1out, r2in, r2out, zsend, r3,
    part, partr, vown, vcore, vy, vx, vz,
    cs, cr, zs, zr, ws, wr, g1is, g1ir, g1os, g1or, g2s, g2r, g3s, g3r, ps, pr, vs, vr, ls,
):
    x, y, z, c = coordinates()
    xp = [lax.rem(x + d, NX) for d in range(NX)]
    yp = [lax.rem(y + d, NY) for d in range(NY)]
    zp = [lax.rem(z + d, NZ) for d in range(NZ)]
    to_x = [device(q, y, z, c) for q in xp]
    to_y = [device(x, q, z, c) for q in yp]
    to_z = [device(x, y, q, c) for q in zp]
    to_c = device(x, y, z, 1 - c)
    pending = []

    def send(src, dst, ssem, rsem, target):
        copy = pltpu.make_async_remote_copy(
            src_ref=src, dst_ref=dst, send_sem=ssem, recv_sem=rsem,
            device_id=target, device_id_type=MESH,
        )
        copy.start()
        pending.append(copy)
        return copy

    barrier = pltpu.get_barrier_semaphore()
    for q in to_x[1:] + to_y[1:] + to_z[1:] + [to_c]:
        pl.semaphore_signal(barrier, inc=1, device_id=q, device_id_type=MESH)

    loads = [
        pltpu.make_async_copy(tok_ref, tokv, ls.at[0]),
        pltpu.make_async_copy(cot_ref, cotv, ls.at[1]),
    ]
    for copy in loads:
        copy.start()
    shard[...] = jnp.zeros_like(shard)
    shard[0:OWN, :] = decode(cin_ref[...], sin_ref[...]).astype(BF)
    shard[16 : 16 + OWN, :] = decode(cout_ref[...], sout_ref[...]).astype(BF)
    zpk[...] = shard_pack(shard)
    zbuf[z] = zpk[...]
    pl.semaphore_wait(barrier, NX + NY + NZ - 2)

    zc = [
        send(zpk, zbuf.at[z], zs.at[d - 1], zr.at[d - 1], to_z[d])
        for d in (4, 3, 5, 2, 6, 1, 7)
    ]
    for copy, buf, ref in zip(loads, (tokb, cotb), (tokv, cotv)):
        copy.wait()
        buf[ROWS - 16 : ROWS, :] = jnp.zeros((16, WIDTH), BF)
        buf[0:FRAMES, :] = ref[0]
    own, other = slice(0, ROWS), slice(ROWS, 2 * ROWS)
    cc = [
        send(buf.at[own], buf.at[other], cs.at[i], cr.at[i], to_c)
        for i, buf in enumerate((tokb, cotb))
    ]

    gain, shift = gain_ref[...].reshape(1, WIDTH), shift_ref[...].reshape(1, WIDTH)

    def norm(rows):
        t = tokb[rows, :].astype(F32)
        t = t - jnp.mean(t, axis=-1, keepdims=True)
        inv = lax.rsqrt(jnp.mean(t * t, axis=-1, keepdims=True) + 1e-05)
        t = t * inv
        normed[rows, :] = (t * gain + shift).astype(BF)
        return t, inv

    t, inv = norm(own)
    xhat[...] = t
    rstd[...] = inv
    group, place = order_mask()
    row = lax.broadcasted_iota(jnp.int32, (128, WIDTH), 0)
    in_group = row == group
    hot = [(row == place + 2 * OWN * p).astype(F32) for p in range(4)]
    bias = jnp.zeros((128, 128), F32)
    for p in range(4):
        line = bin_ref[pl.ds(p * WIDTH, WIDTH)].reshape(1, WIDTH)
        bias = bias + dot_exact(hot[p], jnp.where(in_group, line, 0.0), ((1,), (1,)))
    for yy in range(NY):
        for xx in range(NX):
            g = group_of(xx, yy, 0)
            bcol[(yy * NX + xx) * CHUNK : (yy * NX + xx + 1) * CHUNK, :] = jnp.where(
                c == 0, bias[:CHUNK, g : g + 1], bias[:CHUNK, g + 1 : g + 2]
            )
    fill_select(sel)
    for copy in cc:
        copy.wait_recv()
    norm(other)

    for copy in zc:
        copy.wait_recv()
    lines = zbuf[...].reshape(NZ * PACK, 128)
    for j in range(5):
        w = dot_nn(sel[j], lines).astype(BF)
        win[y, x, :, 128 * j : 128 * j + 128] = w[:CHUNK]
        wout[y, x, :, 128 * j : 128 * j + 128] = w[CHUNK:]

    to = ((to_x[1], to_x[3]), (to_y[1], to_y[3]))

    class Item:
        def __init__(self, index, axis, slot, half):
            self.index, self.axis, self.half = index, axis, half
            self.at = [slot(d) for d in range(4)]
            self.copies = [None] * 4

        def go(self, k, ref):
            self.copies[k] = send(ref, ref, ws.at[self.index, k], wr.at[self.index, k], to[self.axis][k % 2])

        def start(self):
            self.go(0, self.at[0])
            self.go(1, self.at[0])

        def forward(self, k):
            self.copies[k].wait_recv()
            if k == 0:
                self.go(2, self.at[3].at[0 : self.half])
            else:
                self.go(3, self.at[1].at[self.half : CHUNK])

        def finish(self):
            self.copies[2].wait_recv()
            self.copies[3].wait_recv()

    first_in = Item(0, 0, lambda d: win.at[y, xp[d]], 48)
    first_out = Item(1, 1, lambda d: wout.at[yp[d], x], 48)
    later_in = [Item(2 + p, 1, lambda d, p=p: win.at[yp[d], xp[p]], (32, 48)[p % 2]) for p in range(4)]
    later_out = [Item(6 + p, 0, lambda d, p=p: wout.at[yp[p], xp[d]], (32, 48)[p % 2]) for p in range(4)]
    first_in.start()
    first_out.start()
    later_in[0].start()
    later_out[0].start()
    for k, p in ((0, 3), (1, 1)):
        first_in.forward(k)
        first_out.forward(k)
        later_in[p].start()
        later_out[p].start()
    for k in (0, 1):
        later_in[0].forward(k)
        later_out[0].forward(k)
    first_in.finish()
    first_out.finish()
    later_in[2].start()
    later_out[2].start()
    for p in (3, 1):
        for k in (0, 1):
            later_in[p].forward(k)
            later_out[p].forward(k)

    g1i, g1o = ([], []), ({}, {})

    def block(d):
        by = yp[d]
        rows = pl.ds(pl.multiple_of(by * BLOCK, BLOCK), BLOCK)
        v = dot_nt(win[by].reshape(BLOCK, WIDTH), normed[...]) + bcol[rows, :]
        phi = 0.5 * (1.0 + lax.erf(v * 0.7071067811865476))
        slope = phi + v * jnp.exp(-0.5 * v * v) * 0.3989422804014327
        a = (v * phi).astype(BF)
        act[rows, :] = a
        dp = dot_nt(wout[by].reshape(BLOCK, WIDTH), cotb[...]) * slope
        folded = dp[:, 0:128]
        for j in range(1, 6):
            folded = folded + dp[:, 128 * j : 128 * j + 128]
        dbp[rows, :] = folded
        dp = dp.astype(BF)
        dpre[rows, :] = dp
        gin[by] = dot_nn(dp, normed[...]).astype(BF).reshape(NX, CHUNK, WIDTH)
        gout[by] = dot_nn(a, cotb[...]).astype(BF).reshape(NX, CHUNK, WIDTH)

    def block_send(d, h):
        by, cols = yp[d], PARTS[h][0]
        if d:
            g1i[h].append(
                send(
                    gin.at[by, :, :, cols], r1in.at[d - 1, :, :, cols],
                    g1is.at[h, d - 1], g1ir.at[h, d - 1], to_y[d],
                )
            )
        g1o[h][d] = [
            send(
                gout.at[by, xp[e], :, cols], r1out.at[e - 1, by, :, cols],
                g1os.at[h, d, e - 1], g1or.at[h, d, e - 1], to_x[e],
            )
            for e in (2, 1, 3)
        ]

    later_out[0].finish()
    block(0)
    for k in (0, 1):
        later_in[2].forward(k)
        later_out[2].forward(k)
    block_send(0, 0)
    block_send(0, 1)
    for p in (1, 3):
        later_out[p].finish()
        block(p)
        block_send(p, 0)
    later_out[2].finish()
    for p in range(4):
        later_in[p].finish()
    block(2)
    block_send(2, 0)
    for p in (1, 3, 2):
        block_send(p, 1)

    wi = win[...].reshape(HIDDEN, WIDTH)
    wo = wout[...].reshape(HIDDEN, WIDTH)
    pc = []
    part[0, 1] = dot_tn(act[:, other], wo)
    pc.append(send(part.at[0, 1], partr.at[0], ps.at[0], pr.at[0], to_c))
    part[1, 1] = dot_tn(dpre[:, other], wi)
    pc.append(send(part.at[1, 1], partr.at[1], ps.at[1], pr.at[1], to_c))
    part[0, 0] = dot_tn(act[:, own], wo)
    part[1, 0] = dot_tn(dpre[:, own], wi)
    cot = cotb[own, :].astype(F32)
    pc[0].wait_recv()
    layer = tokb[own, :].astype(F32) + (part[0, 0] + partr[0]) + bout_ref[...].reshape(1, WIDTH)
    layv[0] = layer.astype(BF)[0:FRAMES]
    stores = [
        pltpu.make_async_copy(layv, layer_ref, ls.at[2]),
        pltpu.make_async_copy(dtv, dtok_ref, ls.at[3]),
    ]
    stores[0].start()
    pc[1].wait_recv()
    dn = part[1, 0] + partr[1]
    xh = xhat[...]
    dx = dn * gain
    dt = cot + rstd[...] * (
        dx - jnp.mean(dx, axis=-1, keepdims=True) - xh * jnp.mean(dx * xh, axis=-1, keepdims=True)
    )
    dtv[0] = dt.astype(BF)[0:FRAMES]
    stores[1].start()

    lane = lax.broadcasted_iota(jnp.int32, (CHUNK, 128), 1)
    db = jnp.zeros((CHUNK, 128), F32)
    for yy in range(NY):
        for xx in range(NX):
            k = yy * NX + xx
            total = jnp.sum(dbp[k * CHUNK : (k + 1) * CHUNK, :], axis=1, keepdims=True)
            db = jnp.where(lane == group_of(xx, yy, c), total, db)
    for p in range(4):
        line = dot_exact(db, hot[p][:CHUNK], ((0,), (0,)))
        vown[p : p + 1, :] = jnp.sum(jnp.where(in_group, line, 0.0), axis=0, keepdims=True)
    vown[4:5, :] = jnp.sum(dn * xh, axis=0, keepdims=True)
    vown[5:6, :] = jnp.sum(dn, axis=0, keepdims=True)
    vown[6:7, :] = jnp.sum(cot, axis=0, keepdims=True)
    vown[7:8, :] = jnp.zeros((1, WIDTH), F32)
    vc = send(vown, vcore, vs.at[0], vr.at[0], to_c)
    vc.wait_recv()
    vz[z] = vown[...] + vcore[...]
    vzc = [send(vz.at[z], vz.at[z], vs.at[6 + d], vr.at[6 + d], to_z[d]) for d in (4, 3, 5, 2, 6, 1, 7)]

    g2 = ([], [])

    def add_in(h):
        cols = PARTS[h][0]
        for copy in g1i[h]:
            copy.wait_recv()
        for d in (1, 3, 2, 0):
            q = xp[d]
            total = gin[y, q, :, cols].astype(F32)
            for e in range(3):
                total = total + r1in[e, q, :, cols].astype(F32)
            s1in[q, :, cols] = total.astype(BF)
            if d:
                g2[h].append(
                    send(
                        s1in.at[q, :, cols], r2in.at[d - 1, :, cols],
                        g2s.at[h, 0, d - 1], g2r.at[h, 0, d - 1], to_x[d],
                    )
                )

    def add_out(d, h):
        cols = PARTS[h][0]
        for copy in g1o[h][d]:
            copy.wait_recv()
        q = yp[d]
        total = gout[q, x, :, cols].astype(F32)
        for e in range(3):
            total = total + r1out[e, q, :, cols].astype(F32)
        s1out[q, :, cols] = total.astype(BF)
        if d:
            g2[h].append(
                send(
                    s1out.at[q, :, cols], r2out.at[d - 1, :, cols],
                    g2s.at[h, 1, d - 1], g2r.at[h, 1, d - 1], to_y[d],
                )
            )

    for d in (0, 1, 3):
        add_out(d, 0)
    for copy in vzc:
        copy.wait_recv()
    total = vz[0]
    for q in range(1, NZ):
        total = total + vz[q]
    vy[y] = total
    vyc = [send(vy.at[y], vy.at[y], vs.at[d], vr.at[d], to_y[d]) for d in (1, 3, 2)]
    add_in(0)
    add_out(2, 0)
    for d in (0, 1, 3):
        add_out(d, 1)
    add_in(1)
    add_out(2, 1)
    for copy in vyc:
        copy.wait_recv()
    vx[x] = (vy[0] + vy[1]) + (vy[2] + vy[3])
    vxc = [send(vx.at[x], vx.at[x], vs.at[3 + d], vr.at[3 + d], to_x[d]) for d in (1, 3, 2)]

    g3 = []
    for h, (cols, rows, groups) in enumerate(PARTS):
        for copy in g2[h]:
            copy.wait_recv()
        sums = []
        for first, got in ((s1in[x, :, cols], r2in), (s1out[y, :, cols], r2out)):
            total = first.astype(F32)
            for d in range(3):
                total = total + got[d, :, cols].astype(F32)
            sums.append(total.astype(BF))
        both = jnp.concatenate(sums, axis=0)
        packed = jnp.zeros((NZ * PACK, 128), F32)
        for k, j in enumerate(groups):
            packed = packed + dot_tn(sel[j], both[:, 128 * k : 128 * k + 128])
        zsend[:, rows, :] = packed.astype(BF).reshape(NZ, PACK, 128)[:, rows]
        g3 += [
            send(zsend.at[zp[d], rows], r3.at[d - 1, rows], g3s.at[h, d - 1], g3r.at[h, d - 1], to_z[d])
            for d in (4, 3, 5, 2, 6, 1, 7)
        ]
    for copy in vxc:
        copy.wait_recv()
    total = ((vx[0] + vx[1]) + (vx[2] + vx[3])) * (1.0 / math.sqrt(TOKENS))
    for p in range(4):
        obin_ref[pl.ds(p * WIDTH, WIDTH)] = total[p : p + 1].reshape(WIDTH)
    ogain_ref[...] = total[4:5].reshape(WIDTH)
    oshift_ref[...] = total[5:6].reshape(WIDTH)
    obout_ref[...] = total[6:7].reshape(WIDTH)

    for copy in g3:
        copy.wait_recv()
    grad = zsend[z].astype(F32)
    for d in range(NZ - 1):
        grad = grad + r3[d].astype(F32)
    for j in range(5):
        cols = slice(128 * j, 128 * j + 128)
        gradin_ref[:, cols] = grad[PLACE[j] : PLACE[j] + OWN]
        gradout_ref[:, cols] = grad[PLACE[j] + OWN : PLACE[j] + 2 * OWN]
    for copy in stores:
        copy.wait()
    for copy in pending:
        copy.wait_send()


def body(
    tokens, cotangent, codes_in, scales_in, codes_out, scales_out,
    layer_norm_gain, layer_norm_bias, bias_in, bias_out,
    master_in, moment_in, second_in, master_out, moment_out, second_out,
):
    vmem = pl.BlockSpec(memory_space=pltpu.VMEM)
    owned = jax.ShapeDtypeStruct((OWN, WIDTH), F32)
    dma = pltpu.SemaphoreType.DMA
    hbm = pl.BlockSpec(memory_space=pl.ANY)
    rounded = pltpu.VMEM(tokens.shape, BF)
    outs = pl.pallas_call(
        kernel,
        out_shape=[jax.ShapeDtypeStruct(tokens.shape, BF)] * 2
        + [jax.ShapeDtypeStruct((n,), F32) for n in (WIDTH, WIDTH, NC * HIDDEN, WIDTH)]
        + [owned] * 2,
        in_specs=[hbm] * 2 + [vmem] * 8,
        out_specs=[hbm] * 2 + [vmem] * 6,
        scratch_shapes=[rounded] * 4
        + [
            pltpu.VMEM((5, 2 * CHUNK, NZ * PACK), BF),
            pltpu.VMEM((2 * ROWS, WIDTH), BF),
            pltpu.VMEM((2 * ROWS, WIDTH), BF),
            pltpu.VMEM((2 * ROWS, WIDTH), BF),
            pltpu.VMEM((ROWS, WIDTH), F32),
            pltpu.VMEM((ROWS, 1), F32),
            pltpu.VMEM((SHARD, WIDTH), BF),
            pltpu.VMEM((PACK, 128), BF),
            pltpu.VMEM((NZ, PACK, 128), BF),
            pltpu.VMEM((NY, NX, CHUNK, WIDTH), BF),
            pltpu.VMEM((NY, NX, CHUNK, WIDTH), BF),
            pltpu.VMEM((HIDDEN, 1), F32),
            pltpu.VMEM((HIDDEN, 128), F32),
            pltpu.VMEM((HIDDEN, 2 * ROWS), BF),
            pltpu.VMEM((HIDDEN, 2 * ROWS), BF),
            pltpu.VMEM((NY, NX, CHUNK, WIDTH), BF),
            pltpu.VMEM((NY, NX, CHUNK, WIDTH), BF),
            pltpu.VMEM((NY - 1, NX, CHUNK, WIDTH), BF),
            pltpu.VMEM((NX - 1, NY, CHUNK, WIDTH), BF),
            pltpu.VMEM((NX, CHUNK, WIDTH), BF),
            pltpu.VMEM((NY, CHUNK, WIDTH), BF),
            pltpu.VMEM((NX - 1, CHUNK, WIDTH), BF),
            pltpu.VMEM((NY - 1, CHUNK, WIDTH), BF),
            pltpu.VMEM((NZ, PACK, 128), BF),
            pltpu.VMEM((NZ - 1, PACK, 128), BF),
            pltpu.VMEM((2, 2, ROWS, WIDTH), F32),
            pltpu.VMEM((2, ROWS, WIDTH), F32),
            pltpu.VMEM((8, WIDTH), F32),
            pltpu.VMEM((8, WIDTH), F32),
            pltpu.VMEM((NY, 8, WIDTH), F32),
            pltpu.VMEM((NX, 8, WIDTH), F32),
            pltpu.VMEM((NZ, 8, WIDTH), F32),
            dma((2,)), dma((2,)),
            dma((7,)), dma((7,)),
            dma((10, 4)), dma((10, 4)),
            dma((2, 3)), dma((2, 3)),
            dma((2, 4, 3)), dma((2, 4, 3)),
            dma((2, 2, 3)), dma((2, 2, 3)),
            dma((2, 7)), dma((2, 7)),
            dma((2,)), dma((2,)),
            dma((14,)), dma((14,)),
            dma((4,)),
        ],
        compiler_params=pltpu.CompilerParams(
            collective_id=0, has_side_effects=True, vmem_limit_bytes=56 * 2**20
        ),
    )(
        tokens, cotangent, codes_in, scales_in, codes_out, scales_out,
        layer_norm_gain, layer_norm_bias, bias_in, bias_out,
    )
    sums = [total * (1.0 / math.sqrt(TOKENS)) for total in outs[6:]]
    return (
        tuple(outs[:6])
        + adamw(master_in, moment_in, second_in, sums[0])
        + adamw(master_out, moment_out, second_out, sums[1])
    )


def solution(mesh):
    tokens, rows, whole = P("fsdp", "seq", None), P(("fsdp", "seq"), None), P()
    return jax.shard_map(
        body,
        mesh=mesh,
        in_specs=(tokens,) * 2 + (rows,) * 4 + (whole,) * 4 + (rows,) * 6,
        out_specs=(tokens,) * 2 + (whole,) * 4 + (rows,) * 6,
        check_vma=False,
    )
```

```python
import math

import jax
import jax.numpy as jnp
from jax import lax
from jax.experimental import pallas as pl
from jax.experimental.pallas import tpu as pltpu
from jax.sharding import PartitionSpec as P

NX, NY, NZ, NC = 4, 4, 8, 2
WIDTH = 640
OWN = 10
FRAMES = 375
ROWS = 384
CHUNK = NZ * OWN
BLOCK = NX * CHUNK
HIDDEN = NY * BLOCK
PACK = 112
PLACE = (0, 20, 40, 64, 84)
PARTS = ((slice(0, 384), slice(0, 64), (0, 1, 2)), (slice(384, 640), slice(64, 112), (3, 4)))
SHARD = 32
TOKENS = 96000
BF, F32 = jnp.bfloat16, jnp.float32
MESH = pl.DeviceIdType.MESH


def dot_nn(a, b):
    return jnp.dot(a, b, preferred_element_type=F32)


def dot_nt(a, b):
    return lax.dot_general(a, b, (((1,), (1,)), ((), ())), preferred_element_type=F32)


def dot_tn(a, b):
    return lax.dot_general(a, b, (((0,), (0,)), ((), ())), preferred_element_type=F32)


def coordinates():
    f = lax.axis_index("fsdp")
    s = lax.axis_index("seq")
    y = lax.rem(f, 4)
    x_hi = lax.rem(f // 4, 2)
    return x_hi * 2 + s // 2, y, f // 8, lax.rem(s, 2)


def device(x, y, z, c):
    return ((z * 2 + x // 2) * 4 + y, lax.rem(x, 2) * 2 + c)


def decode(codes, scales):
    spread = (
        lax.broadcasted_iota(jnp.int32, (20, WIDTH), 1) // 32
        == lax.broadcasted_iota(jnp.int32, (20, WIDTH), 0)
    )
    k = dot_nn((scales - 118).astype(F32).astype(BF), spread.astype(F32).astype(BF)).astype(jnp.int32)
    negative = codes >= 128
    e = (codes >> 3) & 15
    m = codes & 7
    whole = jnp.where(e > 0, m + 8, m)
    value = (whole << (jnp.maximum(e, 1) + k - 1)).astype(F32) * (2.0**-18)
    return jnp.where(negative, -value, value)


def shard_pack(shard_ref):
    r = lax.broadcasted_iota(jnp.int32, (PACK, SHARD), 0)
    col = lax.broadcasted_iota(jnp.int32, (PACK, SHARD), 1)
    col = jnp.where(col < 16, jnp.where(col < OWN, col, -PACK), jnp.where(col < 16 + OWN, col - 6, -PACK))
    out = jnp.zeros((PACK, 128), F32)
    for j in range(5):
        hot = (r - PLACE[j] == col).astype(F32).astype(BF)
        out = out + dot_nn(hot, shard_ref[:, 128 * j : 128 * j + 128])
    return out.astype(BF)


def fill_select(sel_ref):
    r = lax.broadcasted_iota(jnp.int32, (2 * CHUNK, NZ * PACK), 0)
    col = lax.broadcasted_iota(jnp.int32, (2 * CHUNK, NZ * PACK), 1)
    second = (r >= CHUNK).astype(jnp.int32)
    r = r - CHUNK * second
    z = jnp.zeros_like(r)
    for j in range(1, NZ):
        z = z + (r >= OWN * j).astype(jnp.int32)
    gap = col - (z * (PACK - OWN) + r + OWN * second)
    for j in range(5):
        sel_ref[j] = (gap == PLACE[j]).astype(F32).astype(BF)


def order_mask():
    j = lax.broadcasted_iota(jnp.int32, (128, WIDTH), 1)
    later = (j >= 320).astype(jnp.int32)
    j = j - 320 * later
    group = (j * 6554) >> 16
    return group, later * OWN + j - OWN * group


def group_of(xx, yy, c):
    return ((xx // 2 * 4 + yy) * 2 + xx % 2) * 2 + c


def dot_exact(a, b, dims):
    return lax.dot_general(
        a, b, (dims, ((), ())), preferred_element_type=F32, precision=lax.Precision.HIGHEST
    )


def adamw(master, moment, second, grad):
    new_moment = 0.9 * moment + 0.1 * grad
    new_second = 0.95 * second + 0.05 * grad * grad
    new_master = master - 0.001 * (new_moment / (jnp.sqrt(new_second) + 1e-08) + 0.1 * master)
    return new_master, new_moment, new_second


def kernel(
    tok_ref, cot_ref, cin_ref, sin_ref, cout_ref, sout_ref,
    gain_ref, shift_ref, bin_ref, bout_ref,
    layer_ref, dtok_ref, ogain_ref, oshift_ref, obin_ref, obout_ref, gradin_ref, gradout_ref,
    tokv, cotv, layv, dtv, sel, tokb, cotb, normed, xhat, rstd, shard, zpk, zbuf, win, wout, bcol, dbp, act, dpre,
    gin, gout, r1in, r1out, s1in, s1out, r2in, r2out, zsend, r3,
    part, partr, vown, vcore, vy, vx, vz,
    cs, cr, zs, zr, ws, wr, g1is, g1ir, g1os, g1or, g2s, g2r, g3s, g3r, ps, pr, vs, vr, ls,
):
    x, y, z, c = coordinates()
    xp = [lax.rem(x + d, NX) for d in range(NX)]
    yp = [lax.rem(y + d, NY) for d in range(NY)]
    zp = [lax.rem(z + d, NZ) for d in range(NZ)]
    to_x = [device(q, y, z, c) for q in xp]
    to_y = [device(x, q, z, c) for q in yp]
    to_z = [device(x, y, q, c) for q in zp]
    to_c = device(x, y, z, 1 - c)
    pending = []

    def send(src, dst, ssem, rsem, target):
        copy = pltpu.make_async_remote_copy(
            src_ref=src, dst_ref=dst, send_sem=ssem, recv_sem=rsem,
            device_id=target, device_id_type=MESH,
        )
        copy.start()
        pending.append(copy)
        return copy

    barrier = pltpu.get_barrier_semaphore()
    for q in to_x[1:] + to_y[1:] + to_z[1:] + [to_c]:
        pl.semaphore_signal(barrier, inc=1, device_id=q, device_id_type=MESH)

    loads = [
        pltpu.make_async_copy(tok_ref, tokv, ls.at[0]),
        pltpu.make_async_copy(cot_ref, cotv, ls.at[1]),
    ]
    for copy in loads:
        copy.start()
    shard[...] = jnp.zeros_like(shard)
    shard[0:OWN, :] = decode(cin_ref[...], sin_ref[...]).astype(BF)
    shard[16 : 16 + OWN, :] = decode(cout_ref[...], sout_ref[...]).astype(BF)
    zpk[...] = shard_pack(shard)
    zbuf[z] = zpk[...]
    pl.semaphore_wait(barrier, NX + NY + NZ - 2)

    zc = [
        send(zpk, zbuf.at[z], zs.at[d - 1], zr.at[d - 1], to_z[d])
        for d in (4, 3, 5, 2, 6, 1, 7)
    ]
    for copy, buf, ref in zip(loads, (tokb, cotb), (tokv, cotv)):
        copy.wait()
        buf[ROWS - 16 : ROWS, :] = jnp.zeros((16, WIDTH), BF)
        buf[0:FRAMES, :] = ref[0]
    own, other = slice(0, ROWS), slice(ROWS, 2 * ROWS)
    cc = [
        send(buf.at[own], buf.at[other], cs.at[i], cr.at[i], to_c)
        for i, buf in enumerate((tokb, cotb))
    ]

    gain, shift = gain_ref[...].reshape(1, WIDTH), shift_ref[...].reshape(1, WIDTH)

    def norm(rows):
        t = tokb[rows, :].astype(F32)
        t = t - jnp.mean(t, axis=-1, keepdims=True)
        inv = lax.rsqrt(jnp.mean(t * t, axis=-1, keepdims=True) + 1e-05)
        t = t * inv
        normed[rows, :] = (t * gain + shift).astype(BF)
        return t, inv

    t, inv = norm(own)
    xhat[...] = t
    rstd[...] = inv
    group, place = order_mask()
    row = lax.broadcasted_iota(jnp.int32, (128, WIDTH), 0)
    in_group = row == group
    hot = [(row == place + 2 * OWN * p).astype(F32) for p in range(4)]
    bias = jnp.zeros((128, 128), F32)
    for p in range(4):
        line = bin_ref[pl.ds(p * WIDTH, WIDTH)].reshape(1, WIDTH)
        bias = bias + dot_exact(hot[p], jnp.where(in_group, line, 0.0), ((1,), (1,)))
    for yy in range(NY):
        for xx in range(NX):
            g = group_of(xx, yy, 0)
            bcol[(yy * NX + xx) * CHUNK : (yy * NX + xx + 1) * CHUNK, :] = jnp.where(
                c == 0, bias[:CHUNK, g : g + 1], bias[:CHUNK, g + 1 : g + 2]
            )
    fill_select(sel)
    for copy in cc:
        copy.wait_recv()
    norm(other)

    for copy in zc:
        copy.wait_recv()
    lines = zbuf[...].reshape(NZ * PACK, 128)
    for j in range(5):
        w = dot_nn(sel[j], lines).astype(BF)
        win[y, x, :, 128 * j : 128 * j + 128] = w[:CHUNK]
        wout[y, x, :, 128 * j : 128 * j + 128] = w[CHUNK:]

    to = ((to_x[1], to_x[3]), (to_y[1], to_y[3]))

    class Item:
        def __init__(self, index, axis, slot, half):
            self.index, self.axis, self.half = index, axis, half
            self.at = [slot(d) for d in range(4)]
            self.copies = [None] * 4

        def go(self, k, ref):
            self.copies[k] = send(ref, ref, ws.at[self.index, k], wr.at[self.index, k], to[self.axis][k % 2])

        def start(self):
            self.go(0, self.at[0])
            self.go(1, self.at[0])

        def forward(self, k):
            self.copies[k].wait_recv()
            if k == 0:
                self.go(2, self.at[3].at[0 : self.half])
            else:
                self.go(3, self.at[1].at[self.half : CHUNK])

        def finish(self):
            self.copies[2].wait_recv()
            self.copies[3].wait_recv()

    first_in = Item(0, 0, lambda d: win.at[y, xp[d]], 48)
    first_out = Item(1, 1, lambda d: wout.at[yp[d], x], 48)
    later_in = [Item(2 + p, 1, lambda d, p=p: win.at[yp[d], xp[p]], (32, 48)[p % 2]) for p in range(4)]
    later_out = [Item(6 + p, 0, lambda d, p=p: wout.at[yp[p], xp[d]], (32, 48)[p % 2]) for p in range(4)]
    first_in.start()
    first_out.start()
    later_in[0].start()
    later_out[0].start()
    for k, p in ((0, 3), (1, 1)):
        first_in.forward(k)
        first_out.forward(k)
        later_in[p].start()
        later_out[p].start()
    for k in (0, 1):
        later_in[0].forward(k)
        later_out[0].forward(k)
    first_in.finish()
    first_out.finish()
    later_in[2].start()
    later_out[2].start()
    for p in (3, 1):
        for k in (0, 1):
            later_in[p].forward(k)
            later_out[p].forward(k)

    g1i, g1o = ([], []), ({}, {})

    def block(d):
        by = yp[d]
        rows = pl.ds(pl.multiple_of(by * BLOCK, BLOCK), BLOCK)
        v = dot_nt(win[by].reshape(BLOCK, WIDTH), normed[...]) + bcol[rows, :]
        phi = 0.5 * (1.0 + lax.erf(v * 0.7071067811865476))
        slope = phi + v * jnp.exp(-0.5 * v * v) * 0.3989422804014327
        a = (v * phi).astype(BF)
        act[rows, :] = a
        dp = dot_nt(wout[by].reshape(BLOCK, WIDTH), cotb[...]) * slope
        folded = dp[:, 0:128]
        for j in range(1, 6):
            folded = folded + dp[:, 128 * j : 128 * j + 128]
        dbp[rows, :] = folded
        dp = dp.astype(BF)
        dpre[rows, :] = dp
        gin[by] = dot_nn(dp, normed[...]).astype(BF).reshape(NX, CHUNK, WIDTH)
        gout[by] = dot_nn(a, cotb[...]).astype(BF).reshape(NX, CHUNK, WIDTH)

    def block_send(d, h):
        by, cols = yp[d], PARTS[h][0]
        if d:
            g1i[h].append(
                send(
                    gin.at[by, :, :, cols], r1in.at[d - 1, :, :, cols],
                    g1is.at[h, d - 1], g1ir.at[h, d - 1], to_y[d],
                )
            )
        g1o[h][d] = [
            send(
                gout.at[by, xp[e], :, cols], r1out.at[e - 1, by, :, cols],
                g1os.at[h, d, e - 1], g1or.at[h, d, e - 1], to_x[e],
            )
            for e in (2, 1, 3)
        ]

    later_out[0].finish()
    block(0)
    for k in (0, 1):
        later_in[2].forward(k)
        later_out[2].forward(k)
    block_send(0, 0)
    block_send(0, 1)
    for p in (1, 3):
        later_out[p].finish()
        block(p)
        block_send(p, 0)
    later_out[2].finish()
    for p in range(4):
        later_in[p].finish()
    block(2)
    block_send(2, 0)
    for p in (1, 3, 2):
        block_send(p, 1)

    wi = win[...].reshape(HIDDEN, WIDTH)
    wo = wout[...].reshape(HIDDEN, WIDTH)
    pc = []
    part[0, 1] = dot_tn(act[:, other], wo)
    pc.append(send(part.at[0, 1], partr.at[0], ps.at[0], pr.at[0], to_c))
    part[1, 1] = dot_tn(dpre[:, other], wi)
    pc.append(send(part.at[1, 1], partr.at[1], ps.at[1], pr.at[1], to_c))
    part[0, 0] = dot_tn(act[:, own], wo)
    part[1, 0] = dot_tn(dpre[:, own], wi)
    cot = cotb[own, :].astype(F32)
    pc[0].wait_recv()
    layer = tokb[own, :].astype(F32) + (part[0, 0] + partr[0]) + bout_ref[...].reshape(1, WIDTH)
    layv[0] = layer.astype(BF)[0:FRAMES]
    stores = [
        pltpu.make_async_copy(layv, layer_ref, ls.at[2]),
        pltpu.make_async_copy(dtv, dtok_ref, ls.at[3]),
    ]
    stores[0].start()
    pc[1].wait_recv()
    dn = part[1, 0] + partr[1]
    xh = xhat[...]
    dx = dn * gain
    dt = cot + rstd[...] * (
        dx - jnp.mean(dx, axis=-1, keepdims=True) - xh * jnp.mean(dx * xh, axis=-1, keepdims=True)
    )
    dtv[0] = dt.astype(BF)[0:FRAMES]
    stores[1].start()

    lane = lax.broadcasted_iota(jnp.int32, (CHUNK, 128), 1)
    db = jnp.zeros((CHUNK, 128), F32)
    for yy in range(NY):
        for xx in range(NX):
            k = yy * NX + xx
            total = jnp.sum(dbp[k * CHUNK : (k + 1) * CHUNK, :], axis=1, keepdims=True)
            db = jnp.where(lane == group_of(xx, yy, c), total, db)
    for p in range(4):
        line = dot_exact(db, hot[p][:CHUNK], ((0,), (0,)))
        vown[p : p + 1, :] = jnp.sum(jnp.where(in_group, line, 0.0), axis=0, keepdims=True)
    vown[4:5, :] = jnp.sum(dn * xh, axis=0, keepdims=True)
    vown[5:6, :] = jnp.sum(dn, axis=0, keepdims=True)
    vown[6:7, :] = jnp.sum(cot, axis=0, keepdims=True)
    vown[7:8, :] = jnp.zeros((1, WIDTH), F32)
    vc = send(vown, vcore, vs.at[0], vr.at[0], to_c)
    vc.wait_recv()
    vz[z] = vown[...] + vcore[...]
    vzc = [send(vz.at[z], vz.at[z], vs.at[6 + d], vr.at[6 + d], to_z[d]) for d in (4, 3, 5, 2, 6, 1, 7)]

    g2 = ([], [])

    def add_in(h):
        cols = PARTS[h][0]
        for copy in g1i[h]:
            copy.wait_recv()
        for d in (1, 3, 2, 0):
            q = xp[d]
            total = gin[y, q, :, cols].astype(F32)
            for e in range(3):
                total = total + r1in[e, q, :, cols].astype(F32)
            s1in[q, :, cols] = total.astype(BF)
            if d:
                g2[h].append(
                    send(
                        s1in.at[q, :, cols], r2in.at[d - 1, :, cols],
                        g2s.at[h, 0, d - 1], g2r.at[h, 0, d - 1], to_x[d],
                    )
                )

    def add_out(d, h):
        cols = PARTS[h][0]
        for copy in g1o[h][d]:
            copy.wait_recv()
        q = yp[d]
        total = gout[q, x, :, cols].astype(F32)
        for e in range(3):
            total = total + r1out[e, q, :, cols].astype(F32)
        s1out[q, :, cols] = total.astype(BF)
        if d:
            g2[h].append(
                send(
                    s1out.at[q, :, cols], r2out.at[d - 1, :, cols],
                    g2s.at[h, 1, d - 1], g2r.at[h, 1, d - 1], to_y[d],
                )
            )

    for d in (0, 1, 3):
        add_out(d, 0)
    add_in(0)
    add_out(2, 0)
    for copy in vzc:
        copy.wait_recv()
    total = vz[0]
    for q in range(1, NZ):
        total = total + vz[q]
    vy[y] = total
    vyc = [send(vy.at[y], vy.at[y], vs.at[d], vr.at[d], to_y[d]) for d in (1, 3, 2)]
    for d in (0, 1, 3):
        add_out(d, 1)
    add_in(1)
    add_out(2, 1)
    g3 = []
    for h, (cols, rows, groups) in enumerate(PARTS):
        for copy in g2[h]:
            copy.wait_recv()
        sums = []
        for first, got in ((s1in[x, :, cols], r2in), (s1out[y, :, cols], r2out)):
            total = first.astype(F32)
            for d in range(3):
                total = total + got[d, :, cols].astype(F32)
            sums.append(total.astype(BF))
        both = jnp.concatenate(sums, axis=0)
        packed = jnp.zeros((NZ * PACK, 128), F32)
        for k, j in enumerate(groups):
            packed = packed + dot_tn(sel[j], both[:, 128 * k : 128 * k + 128])
        zsend[:, rows, :] = packed.astype(BF).reshape(NZ, PACK, 128)[:, rows]
        g3 += [
            send(zsend.at[zp[d], rows], r3.at[d - 1, rows], g3s.at[h, d - 1], g3r.at[h, d - 1], to_z[d])
            for d in (4, 3, 5, 2, 6, 1, 7)
        ]
    for copy in vyc:
        copy.wait_recv()
    vx[x] = (vy[0] + vy[1]) + (vy[2] + vy[3])
    vxc = [send(vx.at[x], vx.at[x], vs.at[3 + d], vr.at[3 + d], to_x[d]) for d in (1, 3, 2)]
    for copy in vxc:
        copy.wait_recv()
    total = ((vx[0] + vx[1]) + (vx[2] + vx[3])) * (1.0 / math.sqrt(TOKENS))
    for p in range(4):
        obin_ref[pl.ds(p * WIDTH, WIDTH)] = total[p : p + 1].reshape(WIDTH)
    ogain_ref[...] = total[4:5].reshape(WIDTH)
    oshift_ref[...] = total[5:6].reshape(WIDTH)
    obout_ref[...] = total[6:7].reshape(WIDTH)

    for copy in g3:
        copy.wait_recv()
    grad = zsend[z].astype(F32)
    for d in range(NZ - 1):
        grad = grad + r3[d].astype(F32)
    for j in range(5):
        cols = slice(128 * j, 128 * j + 128)
        gradin_ref[:, cols] = grad[PLACE[j] : PLACE[j] + OWN]
        gradout_ref[:, cols] = grad[PLACE[j] + OWN : PLACE[j] + 2 * OWN]
    for copy in stores:
        copy.wait()
    for copy in pending:
        copy.wait_send()


def body(
    tokens, cotangent, codes_in, scales_in, codes_out, scales_out,
    layer_norm_gain, layer_norm_bias, bias_in, bias_out,
    master_in, moment_in, second_in, master_out, moment_out, second_out,
):
    vmem = pl.BlockSpec(memory_space=pltpu.VMEM)
    owned = jax.ShapeDtypeStruct((OWN, WIDTH), F32)
    dma = pltpu.SemaphoreType.DMA
    hbm = pl.BlockSpec(memory_space=pl.ANY)
    rounded = pltpu.VMEM(tokens.shape, BF)
    outs = pl.pallas_call(
        kernel,
        out_shape=[jax.ShapeDtypeStruct(tokens.shape, BF)] * 2
        + [jax.ShapeDtypeStruct((n,), F32) for n in (WIDTH, WIDTH, NC * HIDDEN, WIDTH)]
        + [owned] * 2,
        in_specs=[hbm] * 2 + [vmem] * 8,
        out_specs=[hbm] * 2 + [vmem] * 6,
        scratch_shapes=[rounded] * 4
        + [
            pltpu.VMEM((5, 2 * CHUNK, NZ * PACK), BF),
            pltpu.VMEM((2 * ROWS, WIDTH), BF),
            pltpu.VMEM((2 * ROWS, WIDTH), BF),
            pltpu.VMEM((2 * ROWS, WIDTH), BF),
            pltpu.VMEM((ROWS, WIDTH), F32),
            pltpu.VMEM((ROWS, 1), F32),
            pltpu.VMEM((SHARD, WIDTH), BF),
            pltpu.VMEM((PACK, 128), BF),
            pltpu.VMEM((NZ, PACK, 128), BF),
            pltpu.VMEM((NY, NX, CHUNK, WIDTH), BF),
            pltpu.VMEM((NY, NX, CHUNK, WIDTH), BF),
            pltpu.VMEM((HIDDEN, 1), F32),
            pltpu.VMEM((HIDDEN, 128), F32),
            pltpu.VMEM((HIDDEN, 2 * ROWS), BF),
            pltpu.VMEM((HIDDEN, 2 * ROWS), BF),
            pltpu.VMEM((NY, NX, CHUNK, WIDTH), BF),
            pltpu.VMEM((NY, NX, CHUNK, WIDTH), BF),
            pltpu.VMEM((NY - 1, NX, CHUNK, WIDTH), BF),
            pltpu.VMEM((NX - 1, NY, CHUNK, WIDTH), BF),
            pltpu.VMEM((NX, CHUNK, WIDTH), BF),
            pltpu.VMEM((NY, CHUNK, WIDTH), BF),
            pltpu.VMEM((NX - 1, CHUNK, WIDTH), BF),
            pltpu.VMEM((NY - 1, CHUNK, WIDTH), BF),
            pltpu.VMEM((NZ, PACK, 128), BF),
            pltpu.VMEM((NZ - 1, PACK, 128), BF),
            pltpu.VMEM((2, 2, ROWS, WIDTH), F32),
            pltpu.VMEM((2, ROWS, WIDTH), F32),
            pltpu.VMEM((8, WIDTH), F32),
            pltpu.VMEM((8, WIDTH), F32),
            pltpu.VMEM((NY, 8, WIDTH), F32),
            pltpu.VMEM((NX, 8, WIDTH), F32),
            pltpu.VMEM((NZ, 8, WIDTH), F32),
            dma((2,)), dma((2,)),
            dma((7,)), dma((7,)),
            dma((10, 4)), dma((10, 4)),
            dma((2, 3)), dma((2, 3)),
            dma((2, 4, 3)), dma((2, 4, 3)),
            dma((2, 2, 3)), dma((2, 2, 3)),
            dma((2, 7)), dma((2, 7)),
            dma((2,)), dma((2,)),
            dma((14,)), dma((14,)),
            dma((4,)),
        ],
        compiler_params=pltpu.CompilerParams(
            collective_id=0, has_side_effects=True, vmem_limit_bytes=56 * 2**20
        ),
    )(
        tokens, cotangent, codes_in, scales_in, codes_out, scales_out,
        layer_norm_gain, layer_norm_bias, bias_in, bias_out,
    )
    sums = [total * (1.0 / math.sqrt(TOKENS)) for total in outs[6:]]
    return (
        tuple(outs[:6])
        + adamw(master_in, moment_in, second_in, sums[0])
        + adamw(master_out, moment_out, second_out, sums[1])
    )


def solution(mesh):
    tokens, rows, whole = P("fsdp", "seq", None), P(("fsdp", "seq"), None), P()
    return jax.shard_map(
        body,
        mesh=mesh,
        in_specs=(tokens,) * 2 + (rows,) * 4 + (whole,) * 4 + (rows,) * 6,
        out_specs=(tokens,) * 2 + (whole,) * 4 + (rows,) * 6,
        check_vma=False,
    )
```

```python
import math

import jax
import jax.numpy as jnp
from jax import lax
from jax.experimental import pallas as pl
from jax.experimental.pallas import tpu as pltpu
from jax.sharding import PartitionSpec as P

NX, NY, NZ, NC = 4, 4, 8, 2
WIDTH = 640
OWN = 10
FRAMES = 375
ROWS = 384
CHUNK = NZ * OWN
BLOCK = NX * CHUNK
HIDDEN = NY * BLOCK
PACK = 112
PLACE = (0, 20, 40, 64, 84)
PARTS = ((slice(0, 384), slice(0, 64), (0, 1, 2)), (slice(384, 640), slice(64, 112), (3, 4)))
SHARD = 32
TOKENS = 96000
BF, F32 = jnp.bfloat16, jnp.float32
MESH = pl.DeviceIdType.MESH


def dot_nn(a, b):
    return jnp.dot(a, b, preferred_element_type=F32)


def dot_nt(a, b):
    return lax.dot_general(a, b, (((1,), (1,)), ((), ())), preferred_element_type=F32)


def dot_tn(a, b):
    return lax.dot_general(a, b, (((0,), (0,)), ((), ())), preferred_element_type=F32)


def coordinates():
    f = lax.axis_index("fsdp")
    s = lax.axis_index("seq")
    y = lax.rem(f, 4)
    x_hi = lax.rem(f // 4, 2)
    return x_hi * 2 + s // 2, y, f // 8, lax.rem(s, 2)


def device(x, y, z, c):
    return ((z * 2 + x // 2) * 4 + y, lax.rem(x, 2) * 2 + c)


def decode(codes, scales):
    spread = (
        lax.broadcasted_iota(jnp.int32, (20, WIDTH), 1) // 32
        == lax.broadcasted_iota(jnp.int32, (20, WIDTH), 0)
    )
    k = dot_nn((scales - 118).astype(F32).astype(BF), spread.astype(F32).astype(BF)).astype(jnp.int32)
    negative = codes >= 128
    e = (codes >> 3) & 15
    m = codes & 7
    whole = jnp.where(e > 0, m + 8, m)
    value = (whole << (jnp.maximum(e, 1) + k - 1)).astype(F32) * (2.0**-18)
    return jnp.where(negative, -value, value)


def shard_pack(shard_ref):
    r = lax.broadcasted_iota(jnp.int32, (PACK, SHARD), 0)
    col = lax.broadcasted_iota(jnp.int32, (PACK, SHARD), 1)
    col = jnp.where(col < 16, jnp.where(col < OWN, col, -PACK), jnp.where(col < 16 + OWN, col - 6, -PACK))
    out = jnp.zeros((PACK, 128), F32)
    for j in range(5):
        hot = (r - PLACE[j] == col).astype(F32).astype(BF)
        out = out + dot_nn(hot, shard_ref[:, 128 * j : 128 * j + 128])
    return out.astype(BF)


def fill_select(sel_ref):
    r = lax.broadcasted_iota(jnp.int32, (2 * CHUNK, NZ * PACK), 0)
    col = lax.broadcasted_iota(jnp.int32, (2 * CHUNK, NZ * PACK), 1)
    second = (r >= CHUNK).astype(jnp.int32)
    r = r - CHUNK * second
    z = jnp.zeros_like(r)
    for j in range(1, NZ):
        z = z + (r >= OWN * j).astype(jnp.int32)
    gap = col - (z * (PACK - OWN) + r + OWN * second)
    for j in range(5):
        sel_ref[j] = (gap == PLACE[j]).astype(F32).astype(BF)


def order_mask():
    j = lax.broadcasted_iota(jnp.int32, (128, WIDTH), 1)
    later = (j >= 320).astype(jnp.int32)
    j = j - 320 * later
    group = (j * 6554) >> 16
    return group, later * OWN + j - OWN * group


def group_of(xx, yy, c):
    return ((xx // 2 * 4 + yy) * 2 + xx % 2) * 2 + c


def dot_exact(a, b, dims):
    return lax.dot_general(
        a, b, (dims, ((), ())), preferred_element_type=F32, precision=lax.Precision.HIGHEST
    )


def adamw(master, moment, second, grad):
    new_moment = 0.9 * moment + 0.1 * grad
    new_second = 0.95 * second + 0.05 * grad * grad
    new_master = master - 0.001 * (new_moment / (jnp.sqrt(new_second) + 1e-08) + 0.1 * master)
    return new_master, new_moment, new_second


def kernel(
    tok_ref, cot_ref, cin_ref, sin_ref, cout_ref, sout_ref,
    gain_ref, shift_ref, bin_ref, bout_ref,
    layer_ref, dtok_ref, ogain_ref, oshift_ref, obin_ref, obout_ref, gradin_ref, gradout_ref,
    tokv, cotv, layv, dtv, sel, tokb, cotb, normed, xhat, rstd, shard, zpk, zbuf, win, wout, bcol, dbp, act, dpre,
    gin, gout, r1in, r1out, s1in, s1out, r2in, r2out, zsend, r3,
    part, partr, vown, vcore, vy, vx, vz,
    cs, cr, zs, zr, ws, wr, g1is, g1ir, g1os, g1or, g2s, g2r, g3s, g3r, ps, pr, vs, vr, ls,
):
    x, y, z, c = coordinates()
    xp = [lax.rem(x + d, NX) for d in range(NX)]
    yp = [lax.rem(y + d, NY) for d in range(NY)]
    zp = [lax.rem(z + d, NZ) for d in range(NZ)]
    to_x = [device(q, y, z, c) for q in xp]
    to_y = [device(x, q, z, c) for q in yp]
    to_z = [device(x, y, q, c) for q in zp]
    to_c = device(x, y, z, 1 - c)
    pending = []

    def send(src, dst, ssem, rsem, target):
        copy = pltpu.make_async_remote_copy(
            src_ref=src, dst_ref=dst, send_sem=ssem, recv_sem=rsem,
            device_id=target, device_id_type=MESH,
        )
        copy.start()
        pending.append(copy)
        return copy

    barrier = pltpu.get_barrier_semaphore()
    for q in to_x[1:] + to_y[1:] + to_z[1:] + [to_c]:
        pl.semaphore_signal(barrier, inc=1, device_id=q, device_id_type=MESH)

    loads = [
        pltpu.make_async_copy(tok_ref, tokv, ls.at[0]),
        pltpu.make_async_copy(cot_ref, cotv, ls.at[1]),
    ]
    for copy in loads:
        copy.start()
    shard[...] = jnp.zeros_like(shard)
    shard[0:OWN, :] = decode(cin_ref[...], sin_ref[...]).astype(BF)
    shard[16 : 16 + OWN, :] = decode(cout_ref[...], sout_ref[...]).astype(BF)
    zpk[...] = shard_pack(shard)
    zbuf[z] = zpk[...]
    pl.semaphore_wait(barrier, NX + NY + NZ - 2)

    zc = [
        send(zpk, zbuf.at[z], zs.at[d - 1], zr.at[d - 1], to_z[d])
        for d in (4, 3, 5, 2, 6, 1, 7)
    ]
    for copy, buf, ref in zip(loads, (tokb, cotb), (tokv, cotv)):
        copy.wait()
        buf[ROWS - 16 : ROWS, :] = jnp.zeros((16, WIDTH), BF)
        buf[0:FRAMES, :] = ref[0]
    own, other = slice(0, ROWS), slice(ROWS, 2 * ROWS)
    cc = [
        send(buf.at[own], buf.at[other], cs.at[i], cr.at[i], to_c)
        for i, buf in enumerate((tokb, cotb))
    ]

    gain, shift = gain_ref[...].reshape(1, WIDTH), shift_ref[...].reshape(1, WIDTH)

    def norm(rows):
        t = tokb[rows, :].astype(F32)
        t = t - jnp.mean(t, axis=-1, keepdims=True)
        inv = lax.rsqrt(jnp.mean(t * t, axis=-1, keepdims=True) + 1e-05)
        t = t * inv
        normed[rows, :] = (t * gain + shift).astype(BF)
        return t, inv

    t, inv = norm(own)
    xhat[...] = t
    rstd[...] = inv
    group, place = order_mask()
    row = lax.broadcasted_iota(jnp.int32, (128, WIDTH), 0)
    in_group = row == group
    hot = [(row == place + 2 * OWN * p).astype(F32) for p in range(4)]
    bias = jnp.zeros((128, 128), F32)
    for p in range(4):
        line = bin_ref[pl.ds(p * WIDTH, WIDTH)].reshape(1, WIDTH)
        bias = bias + dot_exact(hot[p], jnp.where(in_group, line, 0.0), ((1,), (1,)))
    for yy in range(NY):
        for xx in range(NX):
            g = group_of(xx, yy, 0)
            bcol[(yy * NX + xx) * CHUNK : (yy * NX + xx + 1) * CHUNK, :] = jnp.where(
                c == 0, bias[:CHUNK, g : g + 1], bias[:CHUNK, g + 1 : g + 2]
            )
    fill_select(sel)
    for copy in cc:
        copy.wait_recv()
    norm(other)

    for copy in zc:
        copy.wait_recv()
    lines = zbuf[...].reshape(NZ * PACK, 128)
    for j in range(5):
        w = dot_nn(sel[j], lines).astype(BF)
        win[y, x, :, 128 * j : 128 * j + 128] = w[:CHUNK]
        wout[y, x, :, 128 * j : 128 * j + 128] = w[CHUNK:]

    to = ((to_x[1], to_x[3]), (to_y[1], to_y[3]))

    class Item:
        def __init__(self, index, axis, slot, half):
            self.index, self.axis, self.half = index, axis, half
            self.at = [slot(d) for d in range(4)]
            self.copies = [None] * 4

        def go(self, k, ref):
            self.copies[k] = send(ref, ref, ws.at[self.index, k], wr.at[self.index, k], to[self.axis][k % 2])

        def start(self):
            self.go(0, self.at[0])
            self.go(1, self.at[0])

        def forward(self, k):
            self.copies[k].wait_recv()
            if k == 0:
                self.go(2, self.at[3].at[0 : self.half])
            else:
                self.go(3, self.at[1].at[self.half : CHUNK])

        def finish(self):
            self.copies[2].wait_recv()
            self.copies[3].wait_recv()

    first_in = Item(0, 0, lambda d: win.at[y, xp[d]], 48)
    first_out = Item(1, 1, lambda d: wout.at[yp[d], x], 48)
    later_in = [Item(2 + p, 1, lambda d, p=p: win.at[yp[d], xp[p]], (32, 48)[p % 2]) for p in range(4)]
    later_out = [Item(6 + p, 0, lambda d, p=p: wout.at[yp[p], xp[d]], (32, 48)[p % 2]) for p in range(4)]
    first_in.start()
    first_out.start()
    later_in[0].start()
    later_out[0].start()
    for k, p in ((0, 3), (1, 1)):
        first_in.forward(k)
        first_out.forward(k)
        later_in[p].start()
        later_out[p].start()
    for k in (0, 1):
        later_in[0].forward(k)
        later_out[0].forward(k)
    first_in.finish()
    first_out.finish()
    later_in[2].start()
    later_out[2].start()
    for p in (3, 1):
        for k in (0, 1):
            later_in[p].forward(k)
            later_out[p].forward(k)

    g1i, g1o = ([], []), ({}, {})

    def block(d):
        by = yp[d]
        rows = pl.ds(pl.multiple_of(by * BLOCK, BLOCK), BLOCK)
        v = dot_nt(win[by].reshape(BLOCK, WIDTH), normed[...]) + bcol[rows, :]
        phi = 0.5 * (1.0 + lax.erf(v * 0.7071067811865476))
        slope = phi + v * jnp.exp(-0.5 * v * v) * 0.3989422804014327
        a = (v * phi).astype(BF)
        act[rows, :] = a
        dp = dot_nt(wout[by].reshape(BLOCK, WIDTH), cotb[...]) * slope
        folded = dp[:, 0:128]
        for j in range(1, 6):
            folded = folded + dp[:, 128 * j : 128 * j + 128]
        dbp[rows, :] = folded
        dp = dp.astype(BF)
        dpre[rows, :] = dp
        gin[by] = dot_nn(dp, normed[...]).astype(BF).reshape(NX, CHUNK, WIDTH)
        gout[by] = dot_nn(a, cotb[...]).astype(BF).reshape(NX, CHUNK, WIDTH)

    def block_send(d, h):
        by, cols = yp[d], PARTS[h][0]
        if d:
            g1i[h].append(
                send(
                    gin.at[by, :, :, cols], r1in.at[d - 1, :, :, cols],
                    g1is.at[h, d - 1], g1ir.at[h, d - 1], to_y[d],
                )
            )
        g1o[h][d] = [
            send(
                gout.at[by, xp[e], :, cols], r1out.at[e - 1, by, :, cols],
                g1os.at[h, d, e - 1], g1or.at[h, d, e - 1], to_x[e],
            )
            for e in (2, 1, 3)
        ]

    later_out[0].finish()
    block(0)
    for k in (0, 1):
        later_in[2].forward(k)
        later_out[2].forward(k)
    block_send(0, 0)
    block_send(0, 1)
    for p in (1, 3):
        later_out[p].finish()
        block(p)
        block_send(p, 0)
    later_out[2].finish()
    for p in range(4):
        later_in[p].finish()
    block(2)
    block_send(2, 0)
    for p in (1, 3, 2):
        block_send(p, 1)

    wi = win[...].reshape(HIDDEN, WIDTH)
    wo = wout[...].reshape(HIDDEN, WIDTH)
    pc = []
    part[0, 1] = dot_tn(act[:, other], wo)
    pc.append(send(part.at[0, 1], partr.at[0], ps.at[0], pr.at[0], to_c))
    part[1, 1] = dot_tn(dpre[:, other], wi)
    pc.append(send(part.at[1, 1], partr.at[1], ps.at[1], pr.at[1], to_c))
    part[0, 0] = dot_tn(act[:, own], wo)
    part[1, 0] = dot_tn(dpre[:, own], wi)
    cot = cotb[own, :].astype(F32)
    pc[0].wait_recv()
    layer = tokb[own, :].astype(F32) + (part[0, 0] + partr[0]) + bout_ref[...].reshape(1, WIDTH)
    layv[0] = layer.astype(BF)[0:FRAMES]
    stores = [
        pltpu.make_async_copy(layv, layer_ref, ls.at[2]),
        pltpu.make_async_copy(dtv, dtok_ref, ls.at[3]),
    ]
    stores[0].start()
    pc[1].wait_recv()
    dn = part[1, 0] + partr[1]
    xh = xhat[...]
    dx = dn * gain
    dt = cot + rstd[...] * (
        dx - jnp.mean(dx, axis=-1, keepdims=True) - xh * jnp.mean(dx * xh, axis=-1, keepdims=True)
    )
    dtv[0] = dt.astype(BF)[0:FRAMES]
    stores[1].start()

    lane = lax.broadcasted_iota(jnp.int32, (CHUNK, 128), 1)
    db = jnp.zeros((CHUNK, 128), F32)
    for yy in range(NY):
        for xx in range(NX):
            k = yy * NX + xx
            total = jnp.sum(dbp[k * CHUNK : (k + 1) * CHUNK, :], axis=1, keepdims=True)
            db = jnp.where(lane == group_of(xx, yy, c), total, db)
    for p in range(4):
        line = dot_exact(db, hot[p][:CHUNK], ((0,), (0,)))
        vown[p : p + 1, :] = jnp.sum(jnp.where(in_group, line, 0.0), axis=0, keepdims=True)
    vown[4:5, :] = jnp.sum(dn * xh, axis=0, keepdims=True)
    vown[5:6, :] = jnp.sum(dn, axis=0, keepdims=True)
    vown[6:7, :] = jnp.sum(cot, axis=0, keepdims=True)
    vown[7:8, :] = jnp.zeros((1, WIDTH), F32)
    vc = send(vown, vcore, vs.at[0], vr.at[0], to_c)
    vc.wait_recv()
    vz[z] = vown[...] + vcore[...]
    vzc = [send(vz.at[z], vz.at[z], vs.at[6 + d], vr.at[6 + d], to_z[d]) for d in (4, 3, 5, 2, 6, 1, 7)]

    g2 = ([], [])

    def add_in(h):
        cols = PARTS[h][0]
        for copy in g1i[h]:
            copy.wait_recv()
        for d in (1, 3, 2, 0):
            q = xp[d]
            total = gin[y, q, :, cols].astype(F32)
            for e in range(3):
                total = total + r1in[e, q, :, cols].astype(F32)
            s1in[q, :, cols] = total.astype(BF)
            if d:
                g2[h].append(
                    send(
                        s1in.at[q, :, cols], r2in.at[d - 1, :, cols],
                        g2s.at[h, 0, d - 1], g2r.at[h, 0, d - 1], to_x[d],
                    )
                )

    def add_out(d, h):
        cols = PARTS[h][0]
        for copy in g1o[h][d]:
            copy.wait_recv()
        q = yp[d]
        total = gout[q, x, :, cols].astype(F32)
        for e in range(3):
            total = total + r1out[e, q, :, cols].astype(F32)
        s1out[q, :, cols] = total.astype(BF)
        if d:
            g2[h].append(
                send(
                    s1out.at[q, :, cols], r2out.at[d - 1, :, cols],
                    g2s.at[h, 1, d - 1], g2r.at[h, 1, d - 1], to_y[d],
                )
            )

    for d in (0, 1, 3):
        add_out(d, 0)
    add_in(0)
    add_out(2, 0)
    for d in (0, 1, 3):
        add_out(d, 1)
    add_in(1)
    add_out(2, 1)
    for copy in vzc:
        copy.wait_recv()
    total = vz[0]
    for q in range(1, NZ):
        total = total + vz[q]
    vy[y] = total
    vyc = [send(vy.at[y], vy.at[y], vs.at[d], vr.at[d], to_y[d]) for d in (1, 3, 2)]

    g3 = []
    for h, (cols, rows, groups) in enumerate(PARTS):
        for copy in g2[h]:
            copy.wait_recv()
        sums = []
        for first, got in ((s1in[x, :, cols], r2in), (s1out[y, :, cols], r2out)):
            total = first.astype(F32)
            for d in range(3):
                total = total + got[d, :, cols].astype(F32)
            sums.append(total.astype(BF))
        both = jnp.concatenate(sums, axis=0)
        packed = jnp.zeros((NZ * PACK, 128), F32)
        for k, j in enumerate(groups):
            packed = packed + dot_tn(sel[j], both[:, 128 * k : 128 * k + 128])
        zsend[:, rows, :] = packed.astype(BF).reshape(NZ, PACK, 128)[:, rows]
        g3 += [
            send(zsend.at[zp[d], rows], r3.at[d - 1, rows], g3s.at[h, d - 1], g3r.at[h, d - 1], to_z[d])
            for d in (4, 3, 5, 2, 6, 1, 7)
        ]
    for copy in vyc:
        copy.wait_recv()
    vx[x] = (vy[0] + vy[1]) + (vy[2] + vy[3])
    vxc = [send(vx.at[x], vx.at[x], vs.at[3 + d], vr.at[3 + d], to_x[d]) for d in (1, 3, 2)]
    for copy in vxc:
        copy.wait_recv()
    total = ((vx[0] + vx[1]) + (vx[2] + vx[3])) * (1.0 / math.sqrt(TOKENS))
    for p in range(4):
        obin_ref[pl.ds(p * WIDTH, WIDTH)] = total[p : p + 1].reshape(WIDTH)
    ogain_ref[...] = total[4:5].reshape(WIDTH)
    oshift_ref[...] = total[5:6].reshape(WIDTH)
    obout_ref[...] = total[6:7].reshape(WIDTH)

    for copy in g3:
        copy.wait_recv()
    grad = zsend[z].astype(F32)
    for d in range(NZ - 1):
        grad = grad + r3[d].astype(F32)
    for j in range(5):
        cols = slice(128 * j, 128 * j + 128)
        gradin_ref[:, cols] = grad[PLACE[j] : PLACE[j] + OWN]
        gradout_ref[:, cols] = grad[PLACE[j] + OWN : PLACE[j] + 2 * OWN]
    for copy in stores:
        copy.wait()
    for copy in pending:
        copy.wait_send()


def body(
    tokens, cotangent, codes_in, scales_in, codes_out, scales_out,
    layer_norm_gain, layer_norm_bias, bias_in, bias_out,
    master_in, moment_in, second_in, master_out, moment_out, second_out,
):
    vmem = pl.BlockSpec(memory_space=pltpu.VMEM)
    owned = jax.ShapeDtypeStruct((OWN, WIDTH), F32)
    dma = pltpu.SemaphoreType.DMA
    hbm = pl.BlockSpec(memory_space=pl.ANY)
    rounded = pltpu.VMEM(tokens.shape, BF)
    outs = pl.pallas_call(
        kernel,
        out_shape=[jax.ShapeDtypeStruct(tokens.shape, BF)] * 2
        + [jax.ShapeDtypeStruct((n,), F32) for n in (WIDTH, WIDTH, NC * HIDDEN, WIDTH)]
        + [owned] * 2,
        in_specs=[hbm] * 2 + [vmem] * 8,
        out_specs=[hbm] * 2 + [vmem] * 6,
        scratch_shapes=[rounded] * 4
        + [
            pltpu.VMEM((5, 2 * CHUNK, NZ * PACK), BF),
            pltpu.VMEM((2 * ROWS, WIDTH), BF),
            pltpu.VMEM((2 * ROWS, WIDTH), BF),
            pltpu.VMEM((2 * ROWS, WIDTH), BF),
            pltpu.VMEM((ROWS, WIDTH), F32),
            pltpu.VMEM((ROWS, 1), F32),
            pltpu.VMEM((SHARD, WIDTH), BF),
            pltpu.VMEM((PACK, 128), BF),
            pltpu.VMEM((NZ, PACK, 128), BF),
            pltpu.VMEM((NY, NX, CHUNK, WIDTH), BF),
            pltpu.VMEM((NY, NX, CHUNK, WIDTH), BF),
            pltpu.VMEM((HIDDEN, 1), F32),
            pltpu.VMEM((HIDDEN, 128), F32),
            pltpu.VMEM((HIDDEN, 2 * ROWS), BF),
            pltpu.VMEM((HIDDEN, 2 * ROWS), BF),
            pltpu.VMEM((NY, NX, CHUNK, WIDTH), BF),
            pltpu.VMEM((NY, NX, CHUNK, WIDTH), BF),
            pltpu.VMEM((NY - 1, NX, CHUNK, WIDTH), BF),
            pltpu.VMEM((NX - 1, NY, CHUNK, WIDTH), BF),
            pltpu.VMEM((NX, CHUNK, WIDTH), BF),
            pltpu.VMEM((NY, CHUNK, WIDTH), BF),
            pltpu.VMEM((NX - 1, CHUNK, WIDTH), BF),
            pltpu.VMEM((NY - 1, CHUNK, WIDTH), BF),
            pltpu.VMEM((NZ, PACK, 128), BF),
            pltpu.VMEM((NZ - 1, PACK, 128), BF),
            pltpu.VMEM((2, 2, ROWS, WIDTH), F32),
            pltpu.VMEM((2, ROWS, WIDTH), F32),
            pltpu.VMEM((8, WIDTH), F32),
            pltpu.VMEM((8, WIDTH), F32),
            pltpu.VMEM((NY, 8, WIDTH), F32),
            pltpu.VMEM((NX, 8, WIDTH), F32),
            pltpu.VMEM((NZ, 8, WIDTH), F32),
            dma((2,)), dma((2,)),
            dma((7,)), dma((7,)),
            dma((10, 4)), dma((10, 4)),
            dma((2, 3)), dma((2, 3)),
            dma((2, 4, 3)), dma((2, 4, 3)),
            dma((2, 2, 3)), dma((2, 2, 3)),
            dma((2, 7)), dma((2, 7)),
            dma((2,)), dma((2,)),
            dma((14,)), dma((14,)),
            dma((4,)),
        ],
        compiler_params=pltpu.CompilerParams(
            collective_id=0, has_side_effects=True, vmem_limit_bytes=56 * 2**20
        ),
    )(
        tokens, cotangent, codes_in, scales_in, codes_out, scales_out,
        layer_norm_gain, layer_norm_bias, bias_in, bias_out,
    )
    sums = [total * (1.0 / math.sqrt(TOKENS)) for total in outs[6:]]
    return (
        tuple(outs[:6])
        + adamw(master_in, moment_in, second_in, sums[0])
        + adamw(master_out, moment_out, second_out, sums[1])
    )


def solution(mesh):
    tokens, rows, whole = P("fsdp", "seq", None), P(("fsdp", "seq"), None), P()
    return jax.shard_map(
        body,
        mesh=mesh,
        in_specs=(tokens,) * 2 + (rows,) * 4 + (whole,) * 4 + (rows,) * 6,
        out_specs=(tokens,) * 2 + (whole,) * 4 + (rows,) * 6,
        check_vma=False,
    )
```
